256 devices in a mesh: expert: 32 (over z, x_hi, core), pipe: 4 (over y), dp: 2 (over x_lo).
Axes of the slice: x: 4 (x_hi: 2, x_lo: 2; x = x_hi * 2 + x_lo), y: 4, z: 8, core: 2. Of those that a mesh axis runs over, the one named last changes fastest.
Arguments:
- tokens: bfloat16 [4096, 3584], P('expert', ('pipe', 'dp')), may hold values from -6 to 6
- routing: int32 [4096, 8], P('expert'), may hold values from 0 to 31, all different within a row; in each aligned block of 128 rows (0 to 127, 128 to 255, ...) at most 48 rows name the same one
- gate_weights: float32 [4096, 8], P('expert'), may hold values from 0.1 to 0.6
- cotangent: bfloat16 [4096, 3584], P('expert', ('pipe', 'dp')), may hold values from -1.5 to 1.5
- w_in: bfloat16 [32, 3584, 2048], P('expert', ('pipe', 'dp')), may hold values from -0.09375 to 0.09375
- w_out: bfloat16 [32, 1024, 3584], P('expert', None, ('pipe', 'dp')), may hold values from -0.1875 to 0.1875
Outputs:
- mixed: bfloat16 [4096, 3584], P('expert', ('pipe', 'dp'))
- tokens_grad: bfloat16 [4096, 3584], P('expert', ('pipe', 'dp'))
- w_in_grad: bfloat16 [32, 3584, 2048], P('expert', ('pipe', 'dp'))
- w_out_grad: bfloat16 [32, 1024, 3584], P('expert', None, ('pipe', 'dp'))
The draws below stay inside these ranges and needn't reach their ends.
Inputs may be any that keep to these rules, and one draw needn't show every extreme that they name: `routing`: each token names 8 different experts. Among the 128 tokens of one index of the expert axis no expert is named more than 48 times, a bound that some block reaches.
All inputs are finite; a program needn't handle non-finite values.
Results may differ from the reference program's by a relative error of at most 0.029.
Values may be sent and summed in bfloat16 or wider, within the bound.
A program may use at most 128 MiB of HBM per device.

```python
import math
import jax
import jax.numpy as jnp
import numpy as np
from jax import lax

D = 3584
H = 1024
EXPERTS = 32
TOPK = 8
TOK_DEV = 128
CAP = 48
TOKENS = 4096
N_EXPERT = 32
N_PIPE = 4
N_DP = 2


def level_of(own_key, extent, shards, low, top_value):
    def one(axis_at, shards_of):
        steps = jax.random.uniform(jax.random.fold_in(jax.random.fold_in(own_key, 6), axis_at), (shards_of,), jnp.float32, low / len(shards), top_value / len(shards))
        return jnp.repeat(jnp.exp(steps), extent[axis_at] // shards_of).reshape((-1,) + (1,) * (len(extent) - axis_at - 1))

    level = one(*shards[0])
    for cut in shards[1:]:
        level = level * one(*cut)
    return level


def routed_block(own_key, own, number, rows, amount, top, most, lean):
    sequence = jax.random.permutation(own_key, amount)
    heavy_load, common = load_shares(amount, rows * top, most, lean, True), load_shares(amount, rows * top, most, lean, False)
    places = jnp.arange(amount)

    def named(lengths, rotation):
        used = int((lengths > 0).sum())
        fixed = max(1, used // 4)
        passed = fixed + (places - fixed + rotation * (used - fixed)) % max(1, amount - fixed)
        return jnp.zeros((amount,), jnp.int32).at[sequence[jnp.where(places < fixed, places, passed)]].set(jnp.asarray(lengths, jnp.int32))

    lengths = jnp.where(number % 4 == 0, named(heavy_load, number // 4), named(common, number - number // 4 - 1))
    mixed = jax.random.permutation(jax.random.fold_in(own, 3), amount)
    donor, receiver = mixed[0:amount // 2 * 2:2], mixed[1:amount // 2 * 2:2]
    slack = jnp.minimum(lengths[donor] - 1, most - lengths[receiver]) // 2
    slack = jnp.where((donor == sequence[0]) | (receiver == sequence[0]) | (lengths[receiver] == 0), 0, jnp.maximum(slack, 0))
    passed = jax.random.randint(jax.random.fold_in(own, 4), (amount // 2,), 0, 1 << 20) % (slack + 1)
    lengths = lengths.at[donor].add(-passed).at[receiver].add(passed)
    members = jnp.searchsorted(jnp.cumsum(lengths), jnp.arange(rows * top), side="right").astype(jnp.int32)
    grid = members.reshape(top, rows).T
    grid = grid[jax.random.permutation(jax.random.fold_in(own, 1), rows)]
    rotation = jax.random.randint(jax.random.fold_in(own, 2), (rows, 1), 0, top)
    return jnp.take_along_axis(grid, (jnp.arange(top)[None, :] + rotation) % top, axis=1)


def load_shares(number_of, total, reach, skew, full):
    loads = [(1 << 20) // math.isqrt(grade ** skew) + 1 for grade in range(1, number_of + 1)]
    largest = reach if full else min(reach, max(-(-total // number_of), total * loads[0] // sum(loads)))
    least = 1 if total - largest >= number_of - 1 else 0
    holding, surplus = [largest] + [least] * (number_of - 1), total - largest - least * (number_of - 1)
    while surplus > 0:
        candidates = [i for i in range(1, number_of) if holding[i] < largest] or [i for i in range(1, number_of) if holding[i] < reach]
        whole, left = sum([loads[i] for i in candidates]), surplus
        for i in candidates:
            more = min(reach - holding[i], max(1, left * loads[i] // whole), surplus)
            holding[i] = holding[i] + more
            surplus = surplus - more
    return np.array(holding)


def scatter_about(stream_key, shape, deviation, most, cuts=(), kind=jnp.bfloat16):
    gain = level_of(stream_key, shape, cuts, -0.22, 0.18) if cuts else 1.0
    drawn = jax.random.normal(stream_key, shape, jnp.float32) * deviation * gain
    return jnp.minimum(jnp.maximum(drawn, -most), most).astype(kind)


def setup_inputs(seed: int = 0) -> dict:
    arg_keys = jax.random.split(jax.random.key(seed), 7)
    tokens = scatter_about(arg_keys[0], (TOKENS, D), 1.0, 6.0, ((0, 32), (1, 8)))
    routing_keys = jax.random.split(jax.random.fold_in(arg_keys[1], 1), TOKENS // TOK_DEV)
    routing_turns = jax.random.permutation(jax.random.fold_in(arg_keys[1], 3), TOKENS // TOK_DEV)
    routing = jax.vmap(lambda own, number: routed_block(jax.random.fold_in(arg_keys[1], 2), own, number, TOK_DEV, EXPERTS, TOPK, CAP, 2))(routing_keys, routing_turns).reshape((TOKENS, TOPK))
    gate_weights = jnp.clip(0.1 + 0.5 * jax.random.uniform(arg_keys[2], (TOKENS, TOPK), jnp.float32) ** level_of(arg_keys[2], (TOKENS, TOPK), ((0, 32),), -0.2, 0.2), 0.1, 0.6)
    cotangent = scatter_about(arg_keys[3], (TOKENS, D), 0.25, 1.5, ((0, 32), (1, 8)))
    w_in = scatter_about(arg_keys[4], (EXPERTS, D, 2 * H), D ** -0.5, 0.09375, ((0, 32), (1, 8)))
    w_out = scatter_about(arg_keys[5], (EXPERTS, H, D), H ** -0.5, 0.1875, ((0, 32), (2, 8)))
    return {"tokens": tokens, "routing": routing, "gate_weights": gate_weights, "cotangent": cotangent, "w_in": w_in, "w_out": w_out}


def slot_table(routing, experts, capacity):
    count, top = routing.shape
    flat = routing.reshape(count * top).astype(jnp.int32)
    expert_ids = jnp.arange(experts, dtype=jnp.int32)
    onehot = (flat[:, None] == expert_ids[None, :]).astype(jnp.int32)
    earlier = (jnp.cumsum(onehot, axis=0) - onehot).astype(jnp.int32)
    position = jnp.sum(earlier * onehot, axis=1).astype(jnp.int32)
    return (flat * capacity + position).astype(jnp.int32).reshape(count, top)


def silu_parts(gate_pre):
    sigma = jax.nn.sigmoid(gate_pre)
    return gate_pre * sigma, sigma * (1.0 + gate_pre * (1.0 - sigma))


def reference(tokens, routing, gate_weights, cotangent, w_in, w_out):
    groups = N_EXPERT
    blocks = N_PIPE * N_DP
    width = D // blocks
    rows = groups * CAP
    tok_three = tokens.reshape(groups, TOK_DEV, D)
    cot_three = cotangent.reshape(groups, TOK_DEV, D)
    route_three = routing.reshape(groups, TOK_DEV, TOPK)
    gate_three = gate_weights.reshape(groups, TOK_DEV, TOPK)
    slots = jax.vmap(lambda table: slot_table(table, EXPERTS, CAP))(route_three)
    token_ids = jnp.arange(TOK_DEV, dtype=jnp.int32)
    group_ids = jnp.arange(groups, dtype=jnp.int32)[:, None]

    def one_expert(carry, items):
        mixed_acc, grad_acc = carry
        expert, w_first, w_second = items
        cap_ids = (expert * CAP + jnp.arange(CAP, dtype=jnp.int32)).astype(jnp.int32)
        placed = cap_ids[None, :, None, None] == slots[:, None, :, :]
        struck = jnp.any(placed, axis=3)
        valid = jnp.any(struck, axis=2)
        source_tok = jnp.sum(jnp.where(struck, token_ids[None, None, :], 0), axis=2).astype(jnp.int32)
        scale = jnp.sum(jnp.where(placed, gate_three[:, None, :, :], jnp.float32(0.0)), axis=(2, 3))
        zero_row = jnp.zeros((), tokens.dtype)
        x_rows = jnp.where(valid[:, :, None], tok_three[group_ids, source_tok], zero_row).reshape(rows, D)
        dy_rows = (scale[:, :, None] * cot_three[group_ids, source_tok].astype(jnp.float32)).astype(jnp.bfloat16).reshape(rows, D)
        partial_value = jnp.einsum("rfd,fdk->frk", x_rows.reshape(rows, blocks, width).astype(jnp.float32), w_first.reshape(blocks, width, 2 * H).astype(jnp.float32))
        pre = jnp.sum(lax.optimization_barrier(partial_value.astype(jnp.bfloat16)).astype(jnp.float32), axis=0)
        back_part = jnp.einsum("rfd,hfd->frh", dy_rows.reshape(rows, blocks, width).astype(jnp.float32), w_second.reshape(H, blocks, width).astype(jnp.float32))
        back = jnp.sum(lax.optimization_barrier(back_part.astype(jnp.bfloat16)).astype(jnp.float32), axis=0)
        gate_pre = pre[:, :H]
        up_pre = pre[:, H:]
        activated, slope = silu_parts(gate_pre)
        hidden = (activated * up_pre).astype(jnp.bfloat16)
        dgu = jnp.concatenate([back * up_pre * slope, back * activated], axis=1).astype(jnp.bfloat16)
        expert_out = jnp.dot(hidden, w_second, preferred_element_type=jnp.float32).astype(jnp.bfloat16)
        row_grads = jnp.dot(dgu, w_first.T, preferred_element_type=jnp.float32).astype(jnp.bfloat16)
        first_grad = jnp.dot(x_rows.T, dgu, preferred_element_type=jnp.float32).astype(jnp.bfloat16)
        second_grad = jnp.dot(hidden.T, dy_rows, preferred_element_type=jnp.float32).astype(jnp.bfloat16)
        target = (group_ids * TOK_DEV + source_tok).reshape(rows).astype(jnp.int32)
        mixed_acc = mixed_acc.at[target].add(scale.reshape(rows)[:, None] * expert_out.astype(jnp.float32))
        grad_acc = grad_acc.at[target].add(row_grads.astype(jnp.float32))
        return (mixed_acc, grad_acc), (first_grad, second_grad)

    start = (jnp.zeros((TOKENS, D), jnp.float32), jnp.zeros((TOKENS, D), jnp.float32))
    (mixed, tokens_grad), (w_in_grad, w_out_grad) = lax.scan(one_expert, start, (jnp.arange(EXPERTS, dtype=jnp.int32), w_in, w_out))
    return mixed.astype(jnp.bfloat16), tokens_grad.astype(jnp.bfloat16), w_in_grad, w_out_grad
```

```python
import functools

import jax
import jax.numpy as jnp
from jax import lax
from jax.experimental import pallas as pl
from jax.experimental.pallas import tpu as pltpu
from jax.sharding import PartitionSpec as P

H = 1024
CAP = 48
TOK = 128
W = 448
NZ = 8
NQ = 4
NCH = 8
ROWS = NQ * CAP
BW = 384
MESH = pl.DeviceIdType.MESH
F32 = jnp.float32
BF16 = jnp.bfloat16


def nt_dot(a, b):
    return lax.dot_general(a, b, (((1,), (1,)), ((), ())), preferred_element_type=F32)


def tn_dot(a, b):
    return lax.dot_general(a, b, (((0,), (0,)), ((), ())), preferred_element_type=F32)


def dot(a, b):
    return jnp.dot(a, b, preferred_element_type=F32)


def kernel(
    tc_ref,
    rt_ref,
    gt_ref,
    win_hbm,
    wout_ref,
    mixed_ref,
    tgrad_ref,
    wig_ref,
    wog_ref,
    winp,
    code,
    gate,
    x0,
    xr,
    sb,
    r1,
    r2,
    sx,
    rx,
    g,
    outb,
    ret,
    xt,
    acc_in,
    acc_out,
    macc,
    tacc,
    w_sem,
    in_s,
    in_r,
    r1_s,
    r1_r,
    r2_s,
    r2_r,
    x_s,
    x_r,
    gx_s,
    gx_r,
    gd_s,
    gd_r,
    ge_s,
    ge_r,
    gf_s,
    gf_r,
    o_s,
    o_r,
):
    e, p, q = lax.axis_index("expert"), lax.axis_index("pipe"), lax.axis_index("dp")
    z, jm = lax.div(e, NQ), lax.rem(e, NQ)
    pu, pd, pf = lax.rem(p + 1, 4), lax.rem(p + 3, 4), lax.rem(p + 2, 4)
    up, dn, xp = (e, pu, q), (e, pd, q), (e, p, 1 - q)
    qo = 1 - q

    def send(src, dst, ss, rs, dev):
        pltpu.make_async_remote_copy(
            src_ref=src,
            dst_ref=dst,
            send_sem=ss,
            recv_sem=rs,
            device_id=dev,
            device_id_type=MESH,
        ).start()

    def wait(ref, sem):
        pltpu.make_async_copy(ref, ref, sem).wait()

    def shift(c):
        return lax.div(c + 1, 2) * (2 * lax.rem(c, 2) - 1)

    def ahead(c):
        return lax.rem(z + shift(c) + NZ, NZ)

    def behind(c):
        return lax.rem(z - shift(c) + NZ, NZ)

    barrier = pltpu.get_barrier_semaphore()

    @pl.loop(1, 32)
    def _(d):
        pl.semaphore_signal(
            barrier, inc=1, device_id=(lax.rem(e + d, 32), p, q), device_id_type=MESH
        )

    for dev in (up, dn, xp):
        pl.semaphore_signal(barrier, inc=1, device_id=dev, device_id_type=MESH)

    load = pltpu.make_async_copy(win_hbm, winp.at[pl.ds(0, W)], w_sem)
    load.start()
    winp[pl.ds(W, 64), :] = jnp.zeros((64, 2 * H), BF16)
    acc_in[...] = jnp.zeros_like(acc_in)
    acc_out[...] = jnp.zeros_like(acc_out)
    macc[...] = jnp.zeros_like(macc)
    tacc[...] = jnp.zeros_like(tacc)

    ids = lax.broadcasted_iota(jnp.int32, (32, TOK), 0)
    hit = jnp.zeros((32, TOK), F32)
    weight = jnp.zeros((32, TOK), F32)
    for k in range(8):
        same = rt_ref[k : k + 1, :] == ids
        hit = hit + jnp.where(same, 1.0, 0.0)
        weight = weight + jnp.where(same, gt_ref[k : k + 1, :], 0.0)
    before = (
        lax.broadcasted_iota(jnp.int32, (TOK, TOK), 0)
        < lax.broadcasted_iota(jnp.int32, (TOK, TOK), 1)
    )
    slot = dot(hit.astype(BF16), jnp.where(before, 1.0, 0.0).astype(BF16))
    marked = jnp.where(hit > 0.5, slot, -1.0)
    for zz in range(NZ):
        code[zz, :, :] = marked[zz * NQ : zz * NQ + NQ, :]
        gate[zz, :, :] = weight[zz * NQ : zz * NQ + NQ, :]

    row_ids = lax.broadcasted_iota(jnp.int32, (CAP, TOK), 0).astype(F32)

    def picks(zz):
        cq, gq = code[zz], gate[zz]
        chosen = [cq[j : j + 1, :] == row_ids for j in range(NQ)]
        pick = [jnp.where(m, 1.0, 0.0) for m in chosen]
        gates = [jnp.where(m, gq[j : j + 1, :], 0.0) for j, m in enumerate(chosen)]
        return jnp.concatenate(pick, axis=0), jnp.concatenate(gates, axis=0)

    pl.semaphore_wait(barrier, 34)

    lanes = lax.broadcasted_iota(jnp.int32, (ROWS, 2 * W), 1)

    @pl.loop(0, NCH)
    def _(c):
        zz = ahead(c)
        pick, gates = picks(zz)
        row_gate = jnp.sum(gates, axis=1, keepdims=True)
        rows = dot(pick.astype(BF16), tc_ref[...])
        rows = jnp.where(lanes >= W, rows * row_gate, rows).astype(BF16)
        x0[c] = rows.reshape(NQ, CAP, 2 * W)
        for j in range(NQ):
            own = jnp.logical_and(c == 0, jm == j)

            @pl.when(own)
            def _():
                pltpu.make_async_copy(x0.at[c, j], xr.at[c, jm], in_r.at[c]).start()

            @pl.when(jnp.logical_not(own))
            def _():
                send(
                    x0.at[c, j],
                    xr.at[c, jm],
                    in_s.at[c],
                    in_r.at[c],
                    (zz * NQ + j, p, q),
                )

    load.wait()

    def stage_a(c):
        wait(xr.at[c], in_r.at[c])
        rows = xr[c].reshape(ROWS, 2 * W)
        x, dy = rows[:, 0:512], rows[:, 384:896]
        for k, pp in enumerate((pf, pu, pd, p)):
            at = pl.multiple_of(pp * 256, 256)
            gp = dot(x, winp[:, pl.ds(at, 256)]).astype(BF16)
            un = dot(x, winp[:, pl.ds(at + H, 256)]).astype(BF16)
            bk = nt_dot(dy, wout_ref[pl.ds(at, 256), :]).astype(BF16)
            for h in range(2):
                s = slice(h * 128, h * 128 + 128)
                sb[c, pp, h, :, 0:128] = gp[:, s]
                sb[c, pp, h, :, 128:256] = un[:, s]
                sb[c, pp, h, :, 256:384] = bk[:, s]
            if k == 0:
                send(sb.at[c, pf, 0], r1.at[c, 0], r1_s.at[c, 0], r1_r.at[c, 0], up)
                send(sb.at[c, pf, 1], r1.at[c, 1], r1_s.at[c, 1], r1_r.at[c, 1], dn)
            if k == 1:
                send(sb.at[c, pu, 1], r2.at[c, 0], r2_s.at[c, 0], r2_r.at[c, 0], up)
            if k == 2:
                send(sb.at[c, pd, 0], r2.at[c, 1], r2_s.at[c, 1], r2_r.at[c, 1], dn)

    def stage_b(c):
        wait(r1.at[c, 0], r1_r.at[c, 0])
        sb[c, pu, 0] = (sb[c, pu, 0].astype(F32) + r1[c, 0].astype(F32)).astype(BF16)
        send(sb.at[c, pu, 0], r2.at[c, 2], r2_s.at[c, 2], r2_r.at[c, 2], up)
        wait(r1.at[c, 1], r1_r.at[c, 1])
        sb[c, pd, 1] = (sb[c, pd, 1].astype(F32) + r1[c, 1].astype(F32)).astype(BF16)
        send(sb.at[c, pd, 1], r2.at[c, 3], r2_s.at[c, 3], r2_r.at[c, 3], dn)

    def y_sum(c, h):
        return (
            sb[c, p, h].astype(F32)
            + r2[c, 1 - h].astype(F32)
            + r2[c, 2 + h].astype(F32)
        )

    def stage_c(c):
        for k in range(4):
            wait(r2.at[c, k], r2_r.at[c, k])
        sx[c] = y_sum(c, qo).astype(BF16)
        send(sx.at[c], rx.at[c], x_s.at[c], x_r.at[c], xp)

    def stage_d(c):
        wait(rx.at[c], x_r.at[c])
        total = y_sum(c, q) + rx[c].astype(F32)
        gp, un, bk = total[:, 0:128], total[:, 128:256], total[:, 256:384]
        s = 1.0 / (1.0 + jnp.exp(-gp))
        act = gp * s
        g[c, p, q, :, 0:128] = (act * un).astype(BF16)
        g[c, p, q, :, 128:256] = (bk * un * (s * (1.0 + gp * (1.0 - s)))).astype(BF16)
        g[c, p, q, :, 256:384] = (bk * act).astype(BF16)
        mine = g.at[c, p, q]
        send(mine, mine, gx_s.at[c], gx_r.at[c], xp)
        send(mine, mine, gd_s.at[c, 0], gd_r.at[c, 0], up)
        send(mine, mine, gd_s.at[c, 1], gd_r.at[c, 1], dn)

    def stage_e(c):
        other = g.at[c, p, qo]
        wait(other, gx_r.at[c])
        send(other, other, ge_s.at[c, 0], ge_r.at[c, 0], up)
        send(other, other, ge_s.at[c, 1], ge_r.at[c, 1], dn)

    def stage_f(c):
        wait(g.at[c, pd, q], gd_r.at[c, 0])
        wait(g.at[c, pu, q], gd_r.at[c, 1])
        wait(g.at[c, pd, qo], ge_r.at[c, 0])
        wait(g.at[c, pu, qo], ge_r.at[c, 1])
        send(g.at[c, pd, 0], g.at[c, pd, 0], gf_s.at[c, 0], gf_r.at[c, 0], up)
        send(g.at[c, pu, 1], g.at[c, pu, 1], gf_s.at[c, 1], gf_r.at[c, 1], dn)

    def stage_g(c):
        wait(g.at[c, pf, 0], gf_r.at[c, 0])
        wait(g.at[c, pf, 1], gf_r.at[c, 1])

        def part(k):
            s = slice(k * 128, k * 128 + 128)
            return jnp.concatenate(
                [g[c, i // 2, i % 2, :, s] for i in range(8)], axis=1
            )

        back = nt_dot(part(1), winp[:, 0:H]) + nt_dot(part(2), winp[:, H : 2 * H])
        out = dot(part(0), wout_ref[...])
        for j in range(NQ):
            s = slice(j * CAP, j * CAP + CAP)
            outb[c, j, :, 0:384] = back[s, 0:384].astype(BF16)
            outb[c, j, :, 384:512] = (back[s, 384:512] + out[s, 0:128]).astype(BF16)
            outb[c, j, :, 512:896] = out[s, 128:512].astype(BF16)
        zz = behind(c)
        for j in range(NQ):
            own = jnp.logical_and(c == 0, jm == j)

            @pl.when(own)
            def _():
                pltpu.make_async_copy(outb.at[c, j], ret.at[c, jm], o_r.at[c]).start()

            @pl.when(jnp.logical_not(own))
            def _():
                send(
                    outb.at[c, j],
                    ret.at[c, jm],
                    o_s.at[c],
                    o_r.at[c],
                    (zz * NQ + j, p, q),
                )

    def stage_h(c):
        xt[...] = xr[c].reshape(ROWS, 2 * W).T

        @pl.loop(0, 4)
        def _(pp):
            def pair(k):
                s = slice(k * 128, k * 128 + 128)
                return jnp.concatenate([g[c, pp, 0, :, s], g[c, pp, 1, :, s]], axis=1)

            at = pl.multiple_of(pp * 256, 256)
            acc_in[:, pl.ds(at, 256)] += dot(xt[0:512, :], pair(1))
            acc_in[:, pl.ds(at + H, 256)] += dot(xt[0:512, :], pair(2))
            acc_out[:, pl.ds(at, 256)] += dot(xt[384:896, :], pair(0))

    stages = (stage_a, stage_b, stage_c, stage_d, stage_e, stage_f, stage_g)

    @pl.loop(0, NCH + 6)
    def _(s):
        for lag in (5, 4, 3, 2, 1, 0, 6):
            c = s - lag

            @pl.when(jnp.logical_and(c >= 0, c < NCH))
            def _():
                stages[lag](c)

        c = s - 6

        @pl.when(c >= 0)
        def _():
            stage_h(c)

    wig_ref[...] = acc_in[0:W, :].astype(BF16)
    wog_ref[...] = acc_out[...].astype(BF16).T

    @pl.loop(0, NCH)
    def _(c):
        wait(ret.at[c], o_r.at[c])
        pick, gates = picks(ahead(c))
        rows = ret[c].reshape(ROWS, 2 * W)
        high = gates.astype(BF16)
        low = (gates - high.astype(F32)).astype(BF16)
        tacc[...] += tn_dot(pick.astype(BF16), rows[:, 0:512])
        macc[...] += tn_dot(high, rows[:, 384:896]) + tn_dot(low, rows[:, 384:896])

    mixed_ref[...] = macc[...].astype(BF16)
    tgrad_ref[...] = tacc[...].astype(BF16)

    @pl.loop(0, NCH)
    def _(c):
        @pl.when(c == 0)
        def _():
            wait(x0.at[c, pl.ds(0, 3)], in_s.at[c])
            wait(outb.at[c, pl.ds(0, 3)], o_s.at[c])

        @pl.when(c > 0)
        def _():
            wait(x0.at[c], in_s.at[c])
            wait(outb.at[c], o_s.at[c])

        block = sx.at[c]
        for k in range(4):
            wait(block, r2_s.at[c, k])
        wait(block, x_s.at[c])
        wait(block, gx_s.at[c])
        for k in range(2):
            for sem in (r1_s, gd_s, ge_s, gf_s):
                wait(block, sem.at[c, k])


def shards(tokens, routing, gate_weights, cotangent, w_in, w_out):
    both = jnp.concatenate([tokens, cotangent], axis=1)
    wout = jnp.pad(w_out[0], ((0, 0), (64, 0)))
    vmem = pl.BlockSpec(memory_space=pltpu.VMEM)
    dma = pltpu.SemaphoreType.DMA
    mixed, tgrad, wig, wog = pl.pallas_call(
        kernel,
        name="experts",
        out_shape=(
            jax.ShapeDtypeStruct((TOK, 512), BF16),
            jax.ShapeDtypeStruct((TOK, 512), BF16),
            jax.ShapeDtypeStruct((W, 2 * H), BF16),
            jax.ShapeDtypeStruct((H, 512), BF16),
        ),
        in_specs=[vmem, vmem, vmem, pl.BlockSpec(memory_space=pl.ANY), vmem],
        out_specs=(vmem, vmem, vmem, vmem),
        scratch_shapes=[
            pltpu.VMEM((512, 2 * H), BF16),
            pltpu.VMEM((NZ, NQ, TOK), F32),
            pltpu.VMEM((NZ, NQ, TOK), F32),
            pltpu.VMEM((NCH, NQ, CAP, 2 * W), BF16),
            pltpu.VMEM((NCH, NQ, CAP, 2 * W), BF16),
            pltpu.VMEM((NCH, 4, 2, ROWS, BW), BF16),
            pltpu.VMEM((NCH, 2, ROWS, BW), BF16),
            pltpu.VMEM((NCH, 4, ROWS, BW), BF16),
            pltpu.VMEM((NCH, ROWS, BW), BF16),
            pltpu.VMEM((NCH, ROWS, BW), BF16),
            pltpu.VMEM((NCH, 4, 2, ROWS, BW), BF16),
            pltpu.VMEM((NCH, NQ, CAP, 2 * W), BF16),
            pltpu.VMEM((NCH, NQ, CAP, 2 * W), BF16),
            pltpu.VMEM((2 * W, ROWS), BF16),
            pltpu.VMEM((512, 2 * H), F32),
            pltpu.VMEM((512, H), F32),
            pltpu.VMEM((TOK, 512), F32),
            pltpu.VMEM((TOK, 512), F32),
            dma(()),
            dma((NCH,)),
            dma((NCH,)),
            dma((NCH, 2)),
            dma((NCH, 2)),
            dma((NCH, 4)),
            dma((NCH, 4)),
            dma((NCH,)),
            dma((NCH,)),
            dma((NCH,)),
            dma((NCH,)),
            dma((NCH, 2)),
            dma((NCH, 2)),
            dma((NCH, 2)),
            dma((NCH, 2)),
            dma((NCH, 2)),
            dma((NCH, 2)),
            dma((NCH,)),
            dma((NCH,)),
        ],
        compiler_params=pltpu.CompilerParams(
            collective_id=0, has_side_effects=True, vmem_limit_bytes=62 << 20
        ),
    )(both, routing.T, gate_weights.T, w_in[0], wout)
    return mixed[:, 64:], tgrad[:, :W], wig[None], wog[None, :, 64:]


def solution(mesh):
    placed = (
        P("expert", ("pipe", "dp")),
        P("expert", None),
        P("expert", None),
        P("expert", ("pipe", "dp")),
        P("expert", ("pipe", "dp"), None),
        P("expert", None, ("pipe", "dp")),
    )
    return jax.shard_map(
        shards,
        mesh=mesh,
        in_specs=placed,
        out_specs=(
            P("expert", ("pipe", "dp")),
            P("expert", ("pipe", "dp")),
            P("expert", ("pipe", "dp"), None),
            P("expert", None, ("pipe", "dp")),
        ),
        check_vma=False,
    )
```

```python
import jax
import jax.numpy as jnp
from jax import lax
from jax.experimental import pallas as pl
from jax.experimental.pallas import tpu as pltpu
from jax.sharding import PartitionSpec as P

H = 1024
CAP = 48
TOK = 128
W = 448
NZ = 8
NCH = 16
ROWS = 2 * CAP
RY = 80
RX = 16
BW = 384
AHEAD = 3
MESH = pl.DeviceIdType.MESH
F32 = jnp.float32
BF16 = jnp.bfloat16


def nt_dot(a, b):
    return lax.dot_general(a, b, (((1,), (1,)), ((), ())), preferred_element_type=F32)


def tn_dot(a, b):
    return lax.dot_general(a, b, (((0,), (0,)), ((), ())), preferred_element_type=F32)


def dot(a, b):
    return jnp.dot(a, b, preferred_element_type=F32)


def kernel(
    tok_hbm,
    cot_hbm,
    rt_ref,
    gt_ref,
    win_hbm,
    wout_hbm,
    mixed_ref,
    tgrad_ref,
    wig_ref,
    wog_ref,
    tct,
    winp,
    woutp,
    code,
    gate,
    x0,
    xr,
    sb,
    r1,
    r2,
    sx,
    rx,
    g,
    sb2,
    rf,
    q1,
    q2,
    g2,
    outb,
    ret,
    xt,
    acc_in,
    acc_out,
    macc,
    tacc,
    w_sem,
    ss,
    rs,
):
    e, p, q = lax.axis_index("expert"), lax.axis_index("pipe"), lax.axis_index("dp")
    z, xhi, core = lax.div(e, 4), lax.rem(lax.div(e, 2), 2), lax.rem(e, 2)
    pu, pd, pf = lax.rem(p + 1, 4), lax.rem(p + 3, 4), lax.rem(p + 2, 4)
    up, dn, xp = (e, pu, q), (e, pd, q), (e, p, 1 - q)
    qo = 1 - q

    def send(src, dst, c, k, dev):
        pltpu.make_async_remote_copy(
            src_ref=src,
            dst_ref=dst,
            send_sem=ss.at[c, k],
            recv_sem=rs.at[c, k],
            device_id=dev,
            device_id_type=MESH,
        ).start()

    def wait(ref, c, k):
        pltpu.make_async_copy(ref, ref, rs.at[c, k]).wait()

    def place(c, sign):
        i = jnp.where(c == 0, 0, jnp.where(c == NCH - 1, 1, c + 1))
        half = lax.div(i, 2)
        shift = lax.div(half + 1, 2) * (2 * lax.rem(half, 2) - 1)
        zz = lax.rem(z + sign * shift + NZ, NZ)
        return zz * 2 + lax.rem(xhi + lax.rem(i, 2), 2)

    barrier = pltpu.get_barrier_semaphore()

    @pl.loop(1, 32)
    def _(d):
        pl.semaphore_signal(
            barrier, inc=1, device_id=(lax.rem(e + d, 32), p, q), device_id_type=MESH
        )

    for dev in (up, dn, xp):
        pl.semaphore_signal(barrier, inc=1, device_id=dev, device_id_type=MESH)

    loads = [
        pltpu.make_async_copy(tok_hbm, tct.at[pl.ds(0, W)], w_sem.at[0]),
        pltpu.make_async_copy(cot_hbm, tct.at[pl.ds(W, W)], w_sem.at[1]),
        pltpu.make_async_copy(win_hbm, winp.at[pl.ds(0, W)], w_sem.at[2]),
        pltpu.make_async_copy(wout_hbm, woutp.at[pl.ds(64, W)], w_sem.at[3]),
    ]
    for load in loads:
        load.start()
    winp[pl.ds(W, 64), :] = jnp.zeros((64, 2 * H), BF16)
    woutp[pl.ds(0, 64), :] = jnp.zeros((64, H), BF16)

    ids = lax.broadcasted_iota(jnp.int32, (32, TOK), 0)
    hit = jnp.zeros((32, TOK), F32)
    weight = jnp.zeros((32, TOK), F32)
    for k in range(8):
        same = rt_ref[k : k + 1, :] == ids
        hit = hit + jnp.where(same, 1.0, 0.0)
        weight = weight + jnp.where(same, gt_ref[k : k + 1, :], 0.0)
    before = (
        lax.broadcasted_iota(jnp.int32, (TOK, TOK), 0)
        < lax.broadcasted_iota(jnp.int32, (TOK, TOK), 1)
    )
    slot = dot(hit.astype(BF16), jnp.where(before, 1.0, 0.0).astype(BF16))
    marked = jnp.where(hit > 0.5, slot, -1.0)
    for i in range(16):
        code[i, :, :] = marked[2 * i : 2 * i + 2, :]
        gate[i, :, :] = weight[2 * i : 2 * i + 2, :]

    row_ids = lax.broadcasted_iota(jnp.int32, (CAP, TOK), 0).astype(F32)
    lanes = lax.broadcasted_iota(jnp.int32, (ROWS, 2 * W), 1)

    def picks(at):
        cq, gq = code[at], gate[at]
        chosen = [cq[j : j + 1, :] == row_ids for j in range(2)]
        pick = [jnp.where(m, 1.0, 0.0) for m in chosen]
        gates = [jnp.where(m, gq[j : j + 1, :], 0.0) for j, m in enumerate(chosen)]
        return jnp.concatenate(pick, axis=0), jnp.concatenate(gates, axis=0)

    def deliver(src, dst, c, k, at):
        for j in range(2):
            own = jnp.logical_and(c == 0, core == j)

            @pl.when(own)
            def _():
                pltpu.make_async_copy(src.at[c, j], dst.at[c, core], rs.at[c, k]).start()

            @pl.when(jnp.logical_not(own))
            def _():
                send(src.at[c, j], dst.at[c, core], c, k, (at * 2 + j, p, q))

    def stage_pick(c):
        at = place(c, 1)
        pick, gates = picks(at)
        row_gate = jnp.sum(gates, axis=1, keepdims=True)
        rows = nt_dot(pick.astype(BF16), tct[...])
        rows = jnp.where(lanes >= W, rows * row_gate, rows).astype(BF16)
        x0[c] = rows.reshape(2, CAP, 2 * W)
        deliver(x0, xr, c, 0, at)

    def stage_a(c):
        wait(xr.at[c], c, 0)
        rows = xr[c].reshape(ROWS, 2 * W)
        x, dy = rows[:, 0:512], rows[:, 384:896]
        for k, pp in enumerate((pf, pu, pd, p)):
            at = pl.multiple_of(pp * 256, 256)
            gp = dot(x, winp[:, pl.ds(at, 256)]).astype(BF16)
            un = dot(x, winp[:, pl.ds(at + H, 256)]).astype(BF16)
            bk = dot(dy, woutp[:, pl.ds(at, 256)]).astype(BF16)
            for h in range(2):
                s = slice(h * 128, h * 128 + 128)
                for i, v in enumerate((gp, un, bk)):
                    t = slice(i * 128, i * 128 + 128)
                    sb[c, pp, h, :, t] = v[0:RY, s]
                    sb2[c, h, pp, :, t] = v[RY:ROWS, s]
            if k == 0:
                send(sb.at[c, pf, 0], r1.at[c, 0], c, 1, up)
                send(sb.at[c, pf, 1], r1.at[c, 1], c, 2, dn)
            if k == 1:
                send(sb.at[c, pu, 1], r2.at[c, 0], c, 3, up)
            if k == 2:
                send(sb.at[c, pd, 0], r2.at[c, 1], c, 4, dn)
        send(sb2.at[c, qo], rf.at[c], c, 16, xp)

    def by_parity(c, run):
        @pl.when(lax.rem(c, 2) == 0)
        def _():
            run(up, pu, dn, pd)

        @pl.when(lax.rem(c, 2) == 1)
        def _():
            run(dn, pd, up, pu)

    def stage_b(c):
        wait(r1.at[c, 0], c, 1)
        sb[c, pu, 0] = (sb[c, pu, 0].astype(F32) + r1[c, 0].astype(F32)).astype(BF16)
        send(sb.at[c, pu, 0], r2.at[c, 2], c, 5, up)
        wait(r1.at[c, 1], c, 2)
        sb[c, pd, 1] = (sb[c, pd, 1].astype(F32) + r1[c, 1].astype(F32)).astype(BF16)
        send(sb.at[c, pd, 1], r2.at[c, 3], c, 6, dn)
        wait(rf.at[c], c, 16)
        sb2[c, q] = (sb2[c, q].astype(F32) + rf[c].astype(F32)).astype(BF16)

        def run(a, pa, b, pb):
            send(sb2.at[c, q, pf], q1.at[c], c, 17, a)
            send(sb2.at[c, q, pb], q2.at[c, 1], c, 18, b)

        by_parity(c, run)

    def y_sum(c, h):
        return (
            sb[c, p, h].astype(F32)
            + r2[c, 1 - h].astype(F32)
            + r2[c, 2 + h].astype(F32)
        )

    def stage_c(c):
        for k in range(4):
            wait(r2.at[c, k], c, 3 + k)
        sx[c] = y_sum(c, qo).astype(BF16)
        send(sx.at[c], rx.at[c], c, 7, xp)
        wait(q1.at[c], c, 17)

        def run(a, pa, b, pb):
            sb2[c, q, pa] = (sb2[c, q, pa].astype(F32) + q1[c].astype(F32)).astype(BF16)
            send(sb2.at[c, q, pa], q2.at[c, 0], c, 19, a)

        by_parity(c, run)

    def activate(total):
        gp, un, bk = total[:, 0:128], total[:, 128:256], total[:, 256:384]
        s = 1.0 / (1.0 + jnp.exp(-gp))
        act = gp * s
        return jnp.concatenate(
            [act * un, bk * un * (s * (1.0 + gp * (1.0 - s))), bk * act], axis=1
        ).astype(BF16)

    def stage_d(c):
        wait(rx.at[c], c, 7)
        g[c, p, q] = activate(y_sum(c, q) + rx[c].astype(F32))
        mine = g.at[c, p, q]
        send(mine, mine, c, 8, xp)
        send(mine, mine, c, 9, up)
        send(mine, mine, c, 10, dn)
        wait(q2.at[c, 1], c, 18)
        wait(q2.at[c, 0], c, 19)
        g2[c, q, p] = activate(
            sb2[c, q, p].astype(F32) + q2[c, 0].astype(F32) + q2[c, 1].astype(F32)
        )
        mine2 = g2.at[c, q, p]
        send(mine2, mine2, c, 20, up)
        send(mine2, mine2, c, 21, dn)

    def stage_e(c):
        other = g.at[c, p, qo]
        wait(other, c, 8)
        send(other, other, c, 11, up)
        send(other, other, c, 12, dn)
        wait(g2.at[c, q, pd], c, 20)
        wait(g2.at[c, q, pu], c, 21)

        def run(a, pa, b, pb):
            send(g2.at[c, q, pb], g2.at[c, q, pb], c, 22, a)

        by_parity(c, run)

    def stage_f(c):
        wait(g.at[c, pd, q], c, 9)
        wait(g.at[c, pu, q], c, 10)
        wait(g.at[c, pd, qo], c, 11)
        wait(g.at[c, pu, qo], c, 12)
        send(g.at[c, pd, 0], g.at[c, pd, 0], c, 13, up)
        send(g.at[c, pu, 1], g.at[c, pu, 1], c, 14, dn)
        wait(g2.at[c, q, pf], c, 22)
        send(g2.at[c, q], g2.at[c, q], c, 23, xp)

    def stage_g(c):
        wait(g.at[c, pf, 0], c, 13)
        wait(g.at[c, pf, 1], c, 14)
        wait(g2.at[c, qo], c, 23)

        def part(k):
            s = slice(k * 128, k * 128 + 128)
            y = [g[c, i // 2, i % 2, :, s] for i in range(8)]
            x = [g2[c, i % 2, i // 2, :, s] for i in range(8)]
            return jnp.concatenate(
                [jnp.concatenate(y, axis=1), jnp.concatenate(x, axis=1)], axis=0
            )

        back = nt_dot(part(1), winp[:, 0:H]) + nt_dot(part(2), winp[:, H : 2 * H])
        out = nt_dot(part(0), woutp[...])
        for j in range(2):
            s = slice(j * CAP, j * CAP + CAP)
            outb[c, j, :, 0:384] = back[s, 0:384].astype(BF16)
            outb[c, j, :, 384:512] = (back[s, 384:512] + out[s, 0:128]).astype(BF16)
            outb[c, j, :, 512:896] = out[s, 128:512].astype(BF16)
        deliver(outb, ret, c, 15, place(c, -1))

    def stage_h(c):
        xt[...] = xr[c].reshape(ROWS, 2 * W).T

        @pl.loop(0, 4)
        def _(pp):
            def pair(k):
                s = slice(k * 128, k * 128 + 128)
                y = [g[c, pp, h, :, s] for h in range(2)]
                x = [g2[c, h, pp, :, s] for h in range(2)]
                return jnp.concatenate(
                    [jnp.concatenate(y, axis=1), jnp.concatenate(x, axis=1)], axis=0
                )

            at = pl.multiple_of(pp * 256, 256)
            acc_in[:, pl.ds(at, 256)] += dot(xt[0:512, :], pair(1))
            acc_in[:, pl.ds(at + H, 256)] += dot(xt[0:512, :], pair(2))
            acc_out[:, pl.ds(at, 256)] += dot(xt[384:896, :], pair(0))

    def combine(c):
        wait(ret.at[c], c, 15)
        pick, gates = picks(place(c, 1))
        rows = ret[c].reshape(ROWS, 2 * W)
        high = gates.astype(BF16)
        low = (gates - high.astype(F32)).astype(BF16)
        tacc[...] += tn_dot(rows[:, 0:512], pick.astype(BF16))
        macc[...] += tn_dot(rows[:, 384:896], high) + tn_dot(rows[:, 384:896], low)

    loads[0].wait()
    loads[1].wait()
    pl.semaphore_wait(barrier, 34)

    @pl.loop(0, AHEAD)
    def _(c):
        stage_pick(c)

    acc_in[...] = jnp.zeros_like(acc_in)
    acc_out[...] = jnp.zeros_like(acc_out)
    macc[...] = jnp.zeros_like(macc)
    tacc[...] = jnp.zeros_like(tacc)
    loads[2].wait()
    loads[3].wait()

    stages = (
        (stage_f, 5),
        (stage_e, 4),
        (stage_d, 3),
        (stage_c, 2),
        (stage_b, 1),
        (stage_a, 0),
        (stage_pick, -AHEAD),
        (stage_g, 6),
        (stage_h, 6),
        (combine, 8),
    )

    @pl.loop(0, NCH + 6)
    def _(s):
        for stage, lag in stages:
            c = s - lag

            @pl.when(jnp.logical_and(c >= 0, c < NCH))
            def _():
                stage(c)

    wig_ref[...] = acc_in[0:W, :].astype(BF16)
    wog_ref[...] = acc_out[64:512, :].astype(BF16)

    @pl.loop(NCH - 2, NCH)
    def _(c):
        combine(c)

    mixed_ref[...] = macc[64:512, :].astype(BF16)
    tgrad_ref[...] = tacc[0:W, :].astype(BF16)

    def sent(ref, c, k):
        pltpu.make_async_copy(ref, ref, ss.at[c, k]).wait()

    @pl.loop(0, NCH)
    def _(c):
        @pl.when(c == 0)
        def _():
            sent(x0.at[c, 0], c, 0)
            sent(outb.at[c, 0], c, 15)

        @pl.when(c > 0)
        def _():
            sent(x0.at[c], c, 0)
            sent(outb.at[c], c, 15)

        for k in range(1, 15):
            sent(sx.at[c], c, k)
        for k in (16, 23):
            sent(rf.at[c], c, k)
        for k in range(17, 23):
            sent(q1.at[c], c, k)


def shards(tokens, routing, gate_weights, cotangent, w_in, w_out):
    vmem = pl.BlockSpec(memory_space=pltpu.VMEM)
    hbm = pl.BlockSpec(memory_space=pl.ANY)
    dma = pltpu.SemaphoreType.DMA
    mixed, tgrad, wig, wog = pl.pallas_call(
        kernel,
        name="experts",
        out_shape=(
            jax.ShapeDtypeStruct((W, TOK), BF16),
            jax.ShapeDtypeStruct((W, TOK), BF16),
            jax.ShapeDtypeStruct((W, 2 * H), BF16),
            jax.ShapeDtypeStruct((W, H), BF16),
        ),
        in_specs=[hbm, hbm, vmem, vmem, hbm, hbm],
        out_specs=(vmem, vmem, vmem, vmem),
        scratch_shapes=[
            pltpu.VMEM((2 * W, TOK), BF16),
            pltpu.VMEM((512, 2 * H), BF16),
            pltpu.VMEM((512, H), BF16),
            pltpu.VMEM((16, 2, TOK), F32),
            pltpu.VMEM((16, 2, TOK), F32),
            pltpu.VMEM((NCH, 2, CAP, 2 * W), BF16),
            pltpu.VMEM((NCH, 2, CAP, 2 * W), BF16),
            pltpu.VMEM((NCH, 4, 2, RY, BW), BF16),
            pltpu.VMEM((NCH, 2, RY, BW), BF16),
            pltpu.VMEM((NCH, 4, RY, BW), BF16),
            pltpu.VMEM((NCH, RY, BW), BF16),
            pltpu.VMEM((NCH, RY, BW), BF16),
            pltpu.VMEM((NCH, 4, 2, RY, BW), BF16),
            pltpu.VMEM((NCH, 2, 4, RX, BW), BF16),
            pltpu.VMEM((NCH, 4, RX, BW), BF16),
            pltpu.VMEM((NCH, RX, BW), BF16),
            pltpu.VMEM((NCH, 2, RX, BW), BF16),
            pltpu.VMEM((NCH, 2, 4, RX, BW), BF16),
            pltpu.VMEM((NCH, 2, CAP, 2 * W), BF16),
            pltpu.VMEM((NCH, 2, CAP, 2 * W), BF16),
            pltpu.VMEM((2 * W, ROWS), BF16),
            pltpu.VMEM((512, 2 * H), F32),
            pltpu.VMEM((512, H), F32),
            pltpu.VMEM((512, TOK), F32),
            pltpu.VMEM((512, TOK), F32),
            dma((4,)),
            dma((NCH, 24)),
            dma((NCH, 24)),
        ],
        compiler_params=pltpu.CompilerParams(
            collective_id=0, has_side_effects=True, vmem_limit_bytes=62 << 20
        ),
    )(tokens.T, cotangent.T, routing.T, gate_weights.T, w_in[0], w_out[0].T)
    return mixed.T, tgrad.T, wig[None], wog.T[None]


def solution(mesh):
    placed = (
        P("expert", ("pipe", "dp")),
        P("expert", None),
        P("expert", None),
        P("expert", ("pipe", "dp")),
        P("expert", ("pipe", "dp"), None),
        P("expert", None, ("pipe", "dp")),
    )
    return jax.shard_map(
        shards,
        mesh=mesh,
        in_specs=placed,
        out_specs=(
            P("expert", ("pipe", "dp")),
            P("expert", ("pipe", "dp")),
            P("expert", ("pipe", "dp"), None),
            P("expert", None, ("pipe", "dp")),
        ),
        check_vma=False,
    )
```

```python
import jax
import jax.numpy as jnp
from jax import lax
from jax.experimental import pallas as pl
from jax.experimental.pallas import tpu as pltpu
from jax.sharding import PartitionSpec as P

H = 1024
CAP = 48
TOK = 128
W = 448
NZ = 8
NCH = 16
ROWS = 2 * CAP
RY = 64
RX = 32
BW = 384
AHEAD = 3
ORDER = ((0, 0), (2, 0), (-2, 0), (0, 1), (1, 1), (-1, 1), (2, 1), (-2, 1))
ORDER += ((3, 1), (-3, 1), (4, 1), (4, 0), (3, 0), (-3, 0), (1, 0), (-1, 0))
LAST_1 = 10
LOCAL_1 = 3
MESH = pl.DeviceIdType.MESH
F32 = jnp.float32
BF16 = jnp.bfloat16


def nt_dot(a, b):
    return lax.dot_general(a, b, (((1,), (1,)), ((), ())), preferred_element_type=F32)


def tn_dot(a, b):
    return lax.dot_general(a, b, (((0,), (0,)), ((), ())), preferred_element_type=F32)


def dot(a, b):
    return jnp.dot(a, b, preferred_element_type=F32)


def kernel(
    tok_hbm,
    cot_hbm,
    rt_ref,
    gt_ref,
    win_hbm,
    wout_hbm,
    mixed_ref,
    tgrad_ref,
    wig_ref,
    wog_ref,
    tct,
    winp,
    woutp,
    code,
    gate,
    x0,
    xr,
    sb,
    r1,
    r2,
    sx,
    rx,
    g,
    sb2,
    rf,
    q1,
    q2,
    g2,
    outb,
    ret,
    xt,
    acc_in,
    acc_out,
    macc,
    tacc,
    rt2,
    gt2,
    pout,
    pin,
    w_sem,
    ps,
    pr,
    ss,
    rs,
):
    e, p, q = lax.axis_index("expert"), lax.axis_index("pipe"), lax.axis_index("dp")
    z, xhi, core = lax.div(e, 4), lax.rem(lax.div(e, 2), 2), lax.rem(e, 2)
    pu, pd, pf = lax.rem(p + 1, 4), lax.rem(p + 3, 4), lax.rem(p + 2, 4)
    up, dn, xp = (e, pu, q), (e, pd, q), (e, p, 1 - q)
    qo = 1 - q

    def send(src, dst, c, k, dev):
        pltpu.make_async_remote_copy(
            src_ref=src,
            dst_ref=dst,
            send_sem=ss.at[c, k],
            recv_sem=rs.at[c, k],
            device_id=dev,
            device_id_type=MESH,
        ).start()

    def wait(ref, c, k):
        pltpu.make_async_copy(ref, ref, rs.at[c, k]).wait()

    def place(c, sign):
        packed = jnp.int32(0)
        for i, (shift, half) in enumerate(ORDER):
            packed = jnp.where(c == i, 2 * (shift + NZ) + half, packed)
        shift, half = lax.div(packed, 2) - NZ, lax.rem(packed, 2)
        return 2 * lax.rem(z + sign * shift + NZ, NZ) + xhi, half

    barrier = pltpu.get_barrier_semaphore()
    peer = ((2 * z + 1 - xhi) * 2 + core, p, q)

    def greet(dev):
        pl.semaphore_signal(barrier, inc=1, device_id=dev, device_id_type=MESH)

    @pl.loop(0, 16)
    def _(d):
        other = (2 * lax.div(d, 2) + xhi) * 2 + lax.rem(d, 2)

        @pl.when(other != e)
        def _():
            greet((other, p, q))

    for dev in (up, dn, xp, peer):
        greet(dev)

    loads = [
        pltpu.make_async_copy(tok_hbm, tct.at[0, pl.ds(0, W)], w_sem.at[0]),
        pltpu.make_async_copy(cot_hbm, tct.at[0, pl.ds(W, W)], w_sem.at[1]),
        pltpu.make_async_copy(win_hbm, winp.at[pl.ds(0, W)], w_sem.at[2]),
        pltpu.make_async_copy(wout_hbm, woutp.at[pl.ds(64, W)], w_sem.at[3]),
    ]
    for load in loads:
        load.start()
    winp[pl.ds(W, 64), :] = jnp.zeros((64, 2 * H), BF16)
    woutp[pl.ds(0, 64), :] = jnp.zeros((64, H), BF16)

    ids = lax.broadcasted_iota(jnp.int32, (32, TOK), 0)
    before = jnp.where(
        lax.broadcasted_iota(jnp.int32, (TOK, TOK), 0)
        < lax.broadcasted_iota(jnp.int32, (TOK, TOK), 1),
        1.0,
        0.0,
    ).astype(BF16)

    def find_slots(half, rt, gt):
        hit = jnp.zeros((32, TOK), F32)
        weight = jnp.zeros((32, TOK), F32)
        for k in range(8):
            same = rt[k : k + 1, :] == ids
            hit = hit + jnp.where(same, 1.0, 0.0)
            weight = weight + jnp.where(same, gt[k : k + 1, :], 0.0)
        marked = jnp.where(hit > 0.5, dot(hit.astype(BF16), before), -1.0)
        for i in range(16):
            code[half, i, :, :] = marked[2 * i : 2 * i + 2, :]
            gate[half, i, :, :] = weight[2 * i : 2 * i + 2, :]

    find_slots(0, rt_ref, gt_ref)

    row_ids = lax.broadcasted_iota(jnp.int32, (CAP, TOK), 0).astype(F32)
    lanes = lax.broadcasted_iota(jnp.int32, (ROWS, 2 * W), 1)

    def picks(at, half):
        cq, gq = code[half, at], gate[half, at]
        chosen = [cq[j : j + 1, :] == row_ids for j in range(2)]
        pick = [jnp.where(m, 1.0, 0.0) for m in chosen]
        gates = [jnp.where(m, gq[j : j + 1, :], 0.0) for j, m in enumerate(chosen)]
        return jnp.concatenate(pick, axis=0), jnp.concatenate(gates, axis=0)

    def local(c):
        return jnp.logical_or(c == 0, c == LOCAL_1)

    def deliver(src, dst, c, k, at):
        for j in range(2):
            own = jnp.logical_and(local(c), core == j)

            @pl.when(own)
            def _():
                pltpu.make_async_copy(src.at[c, j], dst.at[c, core], rs.at[c, k]).start()

            @pl.when(jnp.logical_not(own))
            def _():
                send(src.at[c, j], dst.at[c, core], c, k, (at * 2 + j, p, q))

    def stage_pick(c):
        at, half = place(c, 1)
        pick, gates = picks(at, half)
        row_gate = jnp.sum(gates, axis=1, keepdims=True)
        rows = nt_dot(pick.astype(BF16), tct[half])
        rows = jnp.where(lanes >= W, rows * row_gate, rows).astype(BF16)
        x0[c] = rows.reshape(2, CAP, 2 * W)
        deliver(x0, xr, c, 0, at)

    def stage_a(c):
        wait(xr.at[c], c, 0)
        rows = xr[c].reshape(ROWS, 2 * W)
        x, dy = rows[:, 0:512], rows[:, 384:896]
        for k, pp in enumerate((pf, pu, pd, p)):
            at = pl.multiple_of(pp * 256, 256)
            gp = dot(x, winp[:, pl.ds(at, 256)]).astype(BF16)
            un = dot(x, winp[:, pl.ds(at + H, 256)]).astype(BF16)
            bk = dot(dy, woutp[:, pl.ds(at, 256)]).astype(BF16)
            for h in range(2):
                s = slice(h * 128, h * 128 + 128)
                for i, v in enumerate((gp, un, bk)):
                    t = slice(i * 128, i * 128 + 128)
                    sb[c, pp, h, :, t] = v[0:RY, s]
                    sb2[c, h, pp, :, t] = v[RY:ROWS, s]
            if k == 0:
                send(sb.at[c, pf, 0], r1.at[c, 0], c, 1, up)
                send(sb.at[c, pf, 1], r1.at[c, 1], c, 2, dn)
            if k == 1:
                send(sb.at[c, pu, 1], r2.at[c, 0], c, 3, up)
            if k == 2:
                send(sb.at[c, pd, 0], r2.at[c, 1], c, 4, dn)
        send(sb2.at[c, qo], rf.at[c], c, 16, xp)

    def by_parity(c, run):
        @pl.when(lax.rem(c, 2) == 0)
        def _():
            run(up, pu, dn, pd)

        @pl.when(lax.rem(c, 2) == 1)
        def _():
            run(dn, pd, up, pu)

    def stage_b(c):
        wait(r1.at[c, 0], c, 1)
        sb[c, pu, 0] = (sb[c, pu, 0].astype(F32) + r1[c, 0].astype(F32)).astype(BF16)
        send(sb.at[c, pu, 0], r2.at[c, 2], c, 5, up)
        wait(r1.at[c, 1], c, 2)
        sb[c, pd, 1] = (sb[c, pd, 1].astype(F32) + r1[c, 1].astype(F32)).astype(BF16)
        send(sb.at[c, pd, 1], r2.at[c, 3], c, 6, dn)
        wait(rf.at[c], c, 16)
        sb2[c, q] = (sb2[c, q].astype(F32) + rf[c].astype(F32)).astype(BF16)

        def run(a, pa, b, pb):
            send(sb2.at[c, q, pf], q1.at[c], c, 17, a)
            send(sb2.at[c, q, pb], q2.at[c, 1], c, 18, b)

        by_parity(c, run)

    def y_sum(c, h):
        return (
            sb[c, p, h].astype(F32)
            + r2[c, 1 - h].astype(F32)
            + r2[c, 2 + h].astype(F32)
        )

    def stage_c(c):
        for k in range(4):
            wait(r2.at[c, k], c, 3 + k)
        sx[c] = y_sum(c, qo).astype(BF16)
        send(sx.at[c], rx.at[c], c, 7, xp)
        wait(q1.at[c], c, 17)

        def run(a, pa, b, pb):
            sb2[c, q, pa] = (sb2[c, q, pa].astype(F32) + q1[c].astype(F32)).astype(BF16)
            send(sb2.at[c, q, pa], q2.at[c, 0], c, 19, a)

        by_parity(c, run)

    def activate(total):
        gp, un, bk = total[:, 0:128], total[:, 128:256], total[:, 256:384]
        s = 1.0 / (1.0 + jnp.exp(-gp))
        act = gp * s
        return jnp.concatenate(
            [act * un, bk * un * (s * (1.0 + gp * (1.0 - s))), bk * act], axis=1
        ).astype(BF16)

    def stage_d(c):
        wait(rx.at[c], c, 7)
        g[c, p, q] = activate(y_sum(c, q) + rx[c].astype(F32))
        mine = g.at[c, p, q]
        send(mine, mine, c, 8, xp)
        send(mine, mine, c, 9, up)
        send(mine, mine, c, 10, dn)
        wait(q2.at[c, 1], c, 18)
        wait(q2.at[c, 0], c, 19)
        g2[c, q, p] = activate(
            sb2[c, q, p].astype(F32) + q2[c, 0].astype(F32) + q2[c, 1].astype(F32)
        )
        mine2 = g2.at[c, q, p]
        send(mine2, mine2, c, 20, up)
        send(mine2, mine2, c, 21, dn)

    def stage_e(c):
        other = g.at[c, p, qo]
        wait(other, c, 8)
        send(other, other, c, 11, up)
        send(other, other, c, 12, dn)
        wait(g2.at[c, q, pd], c, 20)
        wait(g2.at[c, q, pu], c, 21)

        def run(a, pa, b, pb):
            send(g2.at[c, q, pb], g2.at[c, q, pb], c, 22, a)

        by_parity(c, run)

    def stage_f(c):
        wait(g.at[c, pd, q], c, 9)
        wait(g.at[c, pu, q], c, 10)
        wait(g.at[c, pd, qo], c, 11)
        wait(g.at[c, pu, qo], c, 12)
        send(g.at[c, pd, 0], g.at[c, pd, 0], c, 13, up)
        send(g.at[c, pu, 1], g.at[c, pu, 1], c, 14, dn)
        wait(g2.at[c, q, pf], c, 22)
        send(g2.at[c, q], g2.at[c, q], c, 23, xp)

    def stage_g(c):
        wait(g.at[c, pf, 0], c, 13)
        wait(g.at[c, pf, 1], c, 14)
        wait(g2.at[c, qo], c, 23)

        def part(k):
            s = slice(k * 128, k * 128 + 128)
            y = [g[c, i // 2, i % 2, :, s] for i in range(8)]
            x = [g2[c, i % 2, i // 2, :, s] for i in range(8)]
            return jnp.concatenate(
                [jnp.concatenate(y, axis=1), jnp.concatenate(x, axis=1)], axis=0
            )

        back = nt_dot(part(1), winp[:, 0:H]) + nt_dot(part(2), winp[:, H : 2 * H])
        out = nt_dot(part(0), woutp[...])
        for j in range(2):
            s = slice(j * CAP, j * CAP + CAP)
            outb[c, j, :, 0:384] = back[s, 0:384].astype(BF16)
            outb[c, j, :, 384:512] = (back[s, 384:512] + out[s, 0:128]).astype(BF16)
            outb[c, j, :, 512:896] = out[s, 128:512].astype(BF16)
        deliver(outb, ret, c, 15, place(c, -1)[0])

    def stage_h(c):
        xt[...] = xr[c].reshape(ROWS, 2 * W).T

        @pl.loop(0, 4)
        def _(pp):
            def pair(k):
                s = slice(k * 128, k * 128 + 128)
                y = [g[c, pp, h, :, s] for h in range(2)]
                x = [g2[c, h, pp, :, s] for h in range(2)]
                return jnp.concatenate(
                    [jnp.concatenate(y, axis=1), jnp.concatenate(x, axis=1)], axis=0
                )

            at = pl.multiple_of(pp * 256, 256)
            acc_in[:, pl.ds(at, 256)] += dot(xt[0:512, :], pair(1))
            acc_in[:, pl.ds(at + H, 256)] += dot(xt[0:512, :], pair(2))
            acc_out[:, pl.ds(at, 256)] += dot(xt[384:896, :], pair(0))

    def combine(c):
        wait(ret.at[c], c, 15)
        at, half = place(c, 1)
        pick, gates = picks(at, half)
        rows = ret[c].reshape(ROWS, 2 * W)
        high = gates.astype(BF16)
        low = (gates - high.astype(F32)).astype(BF16)
        tacc[half] += tn_dot(rows[:, 0:512], pick.astype(BF16))
        macc[half] += tn_dot(rows[:, 384:896], high) + tn_dot(rows[:, 384:896], low)

    loads[0].wait()
    loads[1].wait()
    pl.semaphore_wait(barrier, 19)

    def to_peer(src, dst, k):
        pltpu.make_async_remote_copy(
            src_ref=src,
            dst_ref=dst,
            send_sem=ps.at[k],
            recv_sem=pr.at[k],
            device_id=peer,
            device_id_type=MESH,
        ).start()

    def peer_wait(ref, sem):
        pltpu.make_async_copy(ref, ref, sem).wait()

    to_peer(rt_ref, rt2, 0)
    to_peer(gt_ref, gt2, 1)
    to_peer(tct.at[0], tct.at[1], 2)

    @pl.loop(0, AHEAD)
    def _(c):
        stage_pick(c)

    acc_in[...] = jnp.zeros_like(acc_in)
    acc_out[...] = jnp.zeros_like(acc_out)
    macc[...] = jnp.zeros_like(macc)
    tacc[...] = jnp.zeros_like(tacc)
    loads[2].wait()
    loads[3].wait()

    stages = (
        (stage_f, 5),
        (stage_e, 4),
        (stage_d, 3),
        (stage_c, 2),
        (stage_b, 1),
        (stage_a, 0),
        (stage_g, 6),
        (stage_h, 6),
        (combine, 8),
    )

    def guarded(stage, c):
        @pl.when(jnp.logical_and(c >= 0, c < NCH))
        def _():
            stage(c)

    @pl.loop(0, NCH + 6)
    def _(s):
        for stage, lag in stages:
            guarded(stage, s - lag)
            if lag == 0:

                @pl.when(s == 0)
                def _():
                    peer_wait(rt2, pr.at[0])
                    peer_wait(gt2, pr.at[1])
                    find_slots(1, rt2, gt2)
                    peer_wait(tct.at[1], pr.at[2])

                for k in range(2):
                    guarded(stage_pick, AHEAD + 2 * s + k)

        @pl.when(s == LAST_1 + 8)
        def _():
            pout[0:W, :] = tacc[1, 0:W, :].astype(BF16)
            pout[W : 2 * W, :] = macc[1, 64:512, :].astype(BF16)
            to_peer(pout, pin, 3)

    wig_ref[...] = acc_in[0:W, :].astype(BF16)
    wog_ref[...] = acc_out[64:512, :].astype(BF16)
    peer_wait(pin, pr.at[3])

    @pl.loop(NCH - 2, NCH)
    def _(c):
        combine(c)

    tgrad_ref[...] = (tacc[0, 0:W, :] + pin[0:W, :].astype(F32)).astype(BF16)
    mixed_ref[...] = (macc[0, 64:512, :] + pin[W : 2 * W, :].astype(F32)).astype(BF16)
    peer_wait(rt2, ps.at[0])
    peer_wait(gt2, ps.at[1])
    peer_wait(pin, ps.at[2])
    peer_wait(pin, ps.at[3])

    def sent(ref, c, k):
        pltpu.make_async_copy(ref, ref, ss.at[c, k]).wait()

    @pl.loop(0, NCH)
    def _(c):
        @pl.when(local(c))
        def _():
            sent(x0.at[c, 0], c, 0)
            sent(outb.at[c, 0], c, 15)

        @pl.when(jnp.logical_not(local(c)))
        def _():
            sent(x0.at[c], c, 0)
            sent(outb.at[c], c, 15)

        for k in range(1, 15):
            sent(sx.at[c], c, k)
        for k in (16, 23):
            sent(rf.at[c], c, k)
        for k in range(17, 23):
            sent(q1.at[c], c, k)


def shards(tokens, routing, gate_weights, cotangent, w_in, w_out):
    vmem = pl.BlockSpec(memory_space=pltpu.VMEM)
    hbm = pl.BlockSpec(memory_space=pl.ANY)
    dma = pltpu.SemaphoreType.DMA
    mixed, tgrad, wig, wog = pl.pallas_call(
        kernel,
        name="experts",
        out_shape=(
            jax.ShapeDtypeStruct((W, TOK), BF16),
            jax.ShapeDtypeStruct((W, TOK), BF16),
            jax.ShapeDtypeStruct((W, 2 * H), BF16),
            jax.ShapeDtypeStruct((W, H), BF16),
        ),
        in_specs=[hbm, hbm, vmem, vmem, hbm, hbm],
        out_specs=(vmem, vmem, vmem, vmem),
        scratch_shapes=[
            pltpu.VMEM((2, 2 * W, TOK), BF16),
            pltpu.VMEM((512, 2 * H), BF16),
            pltpu.VMEM((512, H), BF16),
            pltpu.VMEM((2, 16, 2, TOK), F32),
            pltpu.VMEM((2, 16, 2, TOK), F32),
            pltpu.VMEM((NCH, 2, CAP, 2 * W), BF16),
            pltpu.VMEM((NCH, 2, CAP, 2 * W), BF16),
            pltpu.VMEM((NCH, 4, 2, RY, BW), BF16),
            pltpu.VMEM((NCH, 2, RY, BW), BF16),
            pltpu.VMEM((NCH, 4, RY, BW), BF16),
            pltpu.VMEM((NCH, RY, BW), BF16),
            pltpu.VMEM((NCH, RY, BW), BF16),
            pltpu.VMEM((NCH, 4, 2, RY, BW), BF16),
            pltpu.VMEM((NCH, 2, 4, RX, BW), BF16),
            pltpu.VMEM((NCH, 4, RX, BW), BF16),
            pltpu.VMEM((NCH, RX, BW), BF16),
            pltpu.VMEM((NCH, 2, RX, BW), BF16),
            pltpu.VMEM((NCH, 2, 4, RX, BW), BF16),
            pltpu.VMEM((NCH, 2, CAP, 2 * W), BF16),
            pltpu.VMEM((NCH, 2, CAP, 2 * W), BF16),
            pltpu.VMEM((2 * W, ROWS), BF16),
            pltpu.VMEM((512, 2 * H), F32),
            pltpu.VMEM((512, H), F32),
            pltpu.VMEM((2, 512, TOK), F32),
            pltpu.VMEM((2, 512, TOK), F32),
            pltpu.VMEM((8, TOK), jnp.int32),
            pltpu.VMEM((8, TOK), F32),
            pltpu.VMEM((2 * W, TOK), BF16),
            pltpu.VMEM((2 * W, TOK), BF16),
            dma((4,)),
            dma((4,)),
            dma((4,)),
            dma((NCH, 24)),
            dma((NCH, 24)),
        ],
        compiler_params=pltpu.CompilerParams(
            collective_id=0, has_side_effects=True, vmem_limit_bytes=62 << 20
        ),
    )(tokens.T, cotangent.T, routing.T, gate_weights.T, w_in[0], w_out[0].T)
    return mixed.T, tgrad.T, wig[None], wog.T[None]


def solution(mesh):
    placed = (
        P("expert", ("pipe", "dp")),
        P("expert", None),
        P("expert", None),
        P("expert", ("pipe", "dp")),
        P("expert", ("pipe", "dp"), None),
        P("expert", None, ("pipe", "dp")),
    )
    return jax.shard_map(
        shards,
        mesh=mesh,
        in_specs=placed,
        out_specs=(
            P("expert", ("pipe", "dp")),
            P("expert", ("pipe", "dp")),
            P("expert", ("pipe", "dp"), None),
            P("expert", None, ("pipe", "dp")),
        ),
        check_vma=False,
    )
```

```python
import jax
import jax.numpy as jnp
from jax import lax
from jax.experimental import pallas as pl
from jax.experimental.pallas import tpu as pltpu
from jax.sharding import PartitionSpec as P

H = 1024
CAP = 48
TOK = 128
W = 448
NZ = 8
NCH = 16
ROWS = 2 * CAP
RY = 64
RX = 32
BW = 384
AHEAD = 3
BATCH = 4
LAG = 7
ORDER = ((0, 0), (1, 0), (2, 0), (0, 1), (-1, 1), (3, 1), (-3, 1), (4, 1))
ORDER += ((4, 0), (3, 0), (-3, 0), (2, 1), (-2, 1), (1, 1), (-2, 0), (-1, 0))
LAST_1 = 13
LOCAL_1 = 3
MESH = pl.DeviceIdType.MESH
F32 = jnp.float32
BF16 = jnp.bfloat16


def nt_dot(a, b):
    return lax.dot_general(a, b, (((1,), (1,)), ((), ())), preferred_element_type=F32)


def tn_dot(a, b):
    return lax.dot_general(a, b, (((0,), (0,)), ((), ())), preferred_element_type=F32)


def dot(a, b):
    return jnp.dot(a, b, preferred_element_type=F32)


def kernel(
    tok_hbm,
    cot_hbm,
    rt_ref,
    gt_ref,
    win_hbm,
    wout_hbm,
    mixed_ref,
    tgrad_ref,
    wig_ref,
    wog_ref,
    tct,
    winp,
    woutp,
    code,
    gate,
    x0,
    xr,
    sb,
    r1,
    r2,
    sx,
    rx,
    g,
    sb2,
    rf,
    q1,
    q2,
    g2,
    outb,
    ret,
    xt,
    acc_in,
    acc_out,
    macc,
    tacc,
    rt2,
    gt2,
    pout,
    pin,
    w_sem,
    ps,
    pr,
    ss,
    rs,
):
    e, p, q = lax.axis_index("expert"), lax.axis_index("pipe"), lax.axis_index("dp")
    z, xhi, core = lax.div(e, 4), lax.rem(lax.div(e, 2), 2), lax.rem(e, 2)
    pu, pd, pf = lax.rem(p + 1, 4), lax.rem(p + 3, 4), lax.rem(p + 2, 4)
    up, dn, xp = (e, pu, q), (e, pd, q), (e, p, 1 - q)
    qo = 1 - q

    def send(src, dst, c, k, dev):
        pltpu.make_async_remote_copy(
            src_ref=src,
            dst_ref=dst,
            send_sem=ss.at[c, k],
            recv_sem=rs.at[c, k],
            device_id=dev,
            device_id_type=MESH,
        ).start()

    def wait(ref, c, k):
        pltpu.make_async_copy(ref, ref, rs.at[c, k]).wait()

    def place(c, sign):
        packed = jnp.int32(0)
        for i, (shift, half) in enumerate(ORDER):
            packed = jnp.where(c == i, 2 * (shift + NZ) + half, packed)
        shift, half = lax.div(packed, 2) - NZ, lax.rem(packed, 2)
        return 2 * lax.rem(z + sign * shift + NZ, NZ) + xhi, half

    barrier = pltpu.get_barrier_semaphore()
    peer = ((2 * z + 1 - xhi) * 2 + core, p, q)

    def greet(dev):
        pl.semaphore_signal(barrier, inc=1, device_id=dev, device_id_type=MESH)

    @pl.loop(0, 16)
    def _(d):
        other = (2 * lax.div(d, 2) + xhi) * 2 + lax.rem(d, 2)

        @pl.when(other != e)
        def _():
            greet((other, p, q))

    for dev in (up, dn, xp, peer):
        greet(dev)

    loads = [
        pltpu.make_async_copy(tok_hbm, tct.at[0, pl.ds(0, W)], w_sem.at[0]),
        pltpu.make_async_copy(cot_hbm, tct.at[0, pl.ds(W, W)], w_sem.at[1]),
        pltpu.make_async_copy(win_hbm, winp.at[pl.ds(0, W)], w_sem.at[2]),
        pltpu.make_async_copy(wout_hbm, woutp.at[pl.ds(64, W)], w_sem.at[3]),
    ]
    for load in loads:
        load.start()
    winp[pl.ds(W, 64), :] = jnp.zeros((64, 2 * H), BF16)
    woutp[pl.ds(0, 64), :] = jnp.zeros((64, H), BF16)

    ids = lax.broadcasted_iota(jnp.int32, (32, TOK), 0)
    before = jnp.where(
        lax.broadcasted_iota(jnp.int32, (TOK, TOK), 0)
        < lax.broadcasted_iota(jnp.int32, (TOK, TOK), 1),
        1.0,
        0.0,
    ).astype(BF16)

    def find_slots(half, rt, gt):
        hit = jnp.zeros((32, TOK), F32)
        weight = jnp.zeros((32, TOK), F32)
        for k in range(8):
            same = rt[k : k + 1, :] == ids
            hit = hit + jnp.where(same, 1.0, 0.0)
            weight = weight + jnp.where(same, gt[k : k + 1, :], 0.0)
        marked = jnp.where(hit > 0.5, dot(hit.astype(BF16), before), -1.0)
        for i in range(16):
            code[half, i, :, :] = marked[2 * i : 2 * i + 2, :]
            gate[half, i, :, :] = weight[2 * i : 2 * i + 2, :]

    find_slots(0, rt_ref, gt_ref)

    row_ids = lax.broadcasted_iota(jnp.int32, (CAP, TOK), 0).astype(F32)
    lanes = lax.broadcasted_iota(jnp.int32, (ROWS, 2 * W), 1)

    def picks(at, half):
        cq, gq = code[half, at], gate[half, at]
        chosen = [cq[j : j + 1, :] == row_ids for j in range(2)]
        pick = [jnp.where(m, 1.0, 0.0) for m in chosen]
        gates = [jnp.where(m, gq[j : j + 1, :], 0.0) for j, m in enumerate(chosen)]
        return jnp.concatenate(pick, axis=0), jnp.concatenate(gates, axis=0)

    def local(c):
        return jnp.logical_or(c == 0, c == LOCAL_1)

    def deliver(src, dst, c, k, at):
        for j in range(2):
            own = jnp.logical_and(local(c), core == j)

            @pl.when(own)
            def _():
                pltpu.make_async_copy(src.at[c, j], dst.at[c, core], rs.at[c, k]).start()

            @pl.when(jnp.logical_not(own))
            def _():
                send(src.at[c, j], dst.at[c, core], c, k, (at * 2 + j, p, q))

    def stage_pick(c):
        at, half = place(c, 1)
        pick, gates = picks(at, half)
        row_gate = jnp.sum(gates, axis=1, keepdims=True)
        rows = nt_dot(pick.astype(BF16), tct[half])
        rows = jnp.where(lanes >= W, rows * row_gate, rows).astype(BF16)
        x0[c] = rows.reshape(2, CAP, 2 * W)
        deliver(x0, xr, c, 0, at)

    def stage_a(c):
        wait(xr.at[c], c, 0)
        rows = xr[c].reshape(ROWS, 2 * W)
        x, dy = rows[:, 0:512], rows[:, 384:896]
        for k, pp in enumerate((pf, pu, pd, p)):
            at = pl.multiple_of(pp * 256, 256)
            gp = dot(x, winp[:, pl.ds(at, 256)]).astype(BF16)
            un = dot(x, winp[:, pl.ds(at + H, 256)]).astype(BF16)
            bk = dot(dy, woutp[:, pl.ds(at, 256)]).astype(BF16)
            for h in range(2):
                s = slice(h * 128, h * 128 + 128)
                for i, v in enumerate((gp, un, bk)):
                    t = slice(i * 128, i * 128 + 128)
                    sb[c, pp, h, :, t] = v[0:RY, s]
                    sb2[c, h, pp, :, t] = v[RY:ROWS, s]
            if k == 0:
                send(sb.at[c, pf, 0], r1.at[c, 0], c, 1, up)
                send(sb.at[c, pf, 1], r1.at[c, 1], c, 2, dn)
            if k == 1:
                send(sb.at[c, pu, 1], r2.at[c, 0], c, 3, up)
            if k == 2:
                send(sb.at[c, pd, 0], r2.at[c, 1], c, 4, dn)
        send(sb2.at[c, qo], rf.at[c], c, 16, xp)

    def by_parity(c, run):
        @pl.when(lax.rem(c, 2) == 0)
        def _():
            run(up, pu, dn, pd)

        @pl.when(lax.rem(c, 2) == 1)
        def _():
            run(dn, pd, up, pu)

    def stage_b(c):
        wait(r1.at[c, 0], c, 1)
        sb[c, pu, 0] = (sb[c, pu, 0].astype(F32) + r1[c, 0].astype(F32)).astype(BF16)
        send(sb.at[c, pu, 0], r2.at[c, 2], c, 5, up)
        wait(r1.at[c, 1], c, 2)
        sb[c, pd, 1] = (sb[c, pd, 1].astype(F32) + r1[c, 1].astype(F32)).astype(BF16)
        send(sb.at[c, pd, 1], r2.at[c, 3], c, 6, dn)
        wait(rf.at[c], c, 16)
        sb2[c, q] = (sb2[c, q].astype(F32) + rf[c].astype(F32)).astype(BF16)

        def run(a, pa, b, pb):
            send(sb2.at[c, q, pf], q1.at[c], c, 17, a)
            send(sb2.at[c, q, pb], q2.at[c, 1], c, 18, b)

        by_parity(c, run)

    def y_sum(c, h):
        return (
            sb[c, p, h].astype(F32)
            + r2[c, 1 - h].astype(F32)
            + r2[c, 2 + h].astype(F32)
        )

    def stage_c(c):
        for k in range(4):
            wait(r2.at[c, k], c, 3 + k)
        sx[c] = y_sum(c, qo).astype(BF16)
        send(sx.at[c], rx.at[c], c, 7, xp)
        wait(q1.at[c], c, 17)

        def run(a, pa, b, pb):
            sb2[c, q, pa] = (sb2[c, q, pa].astype(F32) + q1[c].astype(F32)).astype(BF16)
            send(sb2.at[c, q, pa], q2.at[c, 0], c, 19, a)

        by_parity(c, run)

    def activate(total):
        gp, un, bk = total[:, 0:128], total[:, 128:256], total[:, 256:384]
        s = 1.0 / (1.0 + jnp.exp(-gp))
        act = gp * s
        return jnp.concatenate(
            [act * un, bk * un * (s * (1.0 + gp * (1.0 - s))), bk * act], axis=1
        ).astype(BF16)

    def stage_d(c):
        wait(rx.at[c], c, 7)
        g[c, p, q] = activate(y_sum(c, q) + rx[c].astype(F32))
        mine = g.at[c, p, q]
        send(mine, mine, c, 8, xp)
        send(mine, mine, c, 9, up)
        send(mine, mine, c, 10, dn)
        wait(q2.at[c, 1], c, 18)
        wait(q2.at[c, 0], c, 19)
        g2[c, q, p] = activate(
            sb2[c, q, p].astype(F32) + q2[c, 0].astype(F32) + q2[c, 1].astype(F32)
        )
        mine2 = g2.at[c, q, p]
        send(mine2, mine2, c, 20, up)
        send(mine2, mine2, c, 21, dn)

    def stage_e(c):
        other = g.at[c, p, qo]
        wait(other, c, 8)
        send(other, other, c, 11, up)
        send(other, other, c, 12, dn)
        wait(g2.at[c, q, pd], c, 20)
        wait(g2.at[c, q, pu], c, 21)

        def run(a, pa, b, pb):
            send(g2.at[c, q, pb], g2.at[c, q, pb], c, 22, a)

        by_parity(c, run)

    def stage_f(c):
        wait(g.at[c, pd, q], c, 9)
        wait(g.at[c, pu, q], c, 10)
        wait(g.at[c, pd, qo], c, 11)
        wait(g.at[c, pu, qo], c, 12)
        send(g.at[c, pd, 0], g.at[c, pd, 0], c, 13, up)
        send(g.at[c, pu, 1], g.at[c, pu, 1], c, 14, dn)
        wait(g2.at[c, q, pf], c, 22)
        send(g2.at[c, q], g2.at[c, q], c, 23, xp)

    def stage_g(c):
        wait(g.at[c, pf, 0], c, 13)
        wait(g.at[c, pf, 1], c, 14)
        wait(g2.at[c, qo], c, 23)

        def part(k):
            s = slice(k * 128, k * 128 + 128)
            y = [g[c, i // 2, i % 2, :, s] for i in range(8)]
            x = [g2[c, i % 2, i // 2, :, s] for i in range(8)]
            return jnp.concatenate(
                [jnp.concatenate(y, axis=1), jnp.concatenate(x, axis=1)], axis=0
            )

        back = nt_dot(part(1), winp[:, 0:H]) + nt_dot(part(2), winp[:, H : 2 * H])
        out = nt_dot(part(0), woutp[...])
        for j in range(2):
            s = slice(j * CAP, j * CAP + CAP)
            outb[c, j, :, 0:384] = back[s, 0:384].astype(BF16)
            outb[c, j, :, 384:512] = (back[s, 384:512] + out[s, 0:128]).astype(BF16)
            outb[c, j, :, 512:896] = out[s, 128:512].astype(BF16)
        deliver(outb, ret, c, 15, place(c, -1)[0])

    def stage_h(first):
        rows = xr[pl.ds(first, BATCH)].reshape(BATCH * ROWS, 2 * W)
        xt[...] = rows.T

        @pl.loop(0, 4)
        def _(pp):
            def pair(k):
                s = slice(k * 128, k * 128 + 128)
                parts = []
                for b in range(BATCH):
                    c = first + b
                    y = [g[c, pp, h, :, s] for h in range(2)]
                    x = [g2[c, h, pp, :, s] for h in range(2)]
                    parts += [jnp.concatenate(y, axis=1), jnp.concatenate(x, axis=1)]
                return jnp.concatenate(parts, axis=0)

            at = pl.multiple_of(pp * 256, 256)
            acc_in[:, pl.ds(at, 256)] += dot(xt[0:512, :], pair(1))
            acc_in[:, pl.ds(at + H, 256)] += dot(xt[0:512, :], pair(2))
            acc_out[:, pl.ds(at, 256)] += dot(xt[384:896, :], pair(0))

    def combine(c):
        wait(ret.at[c], c, 15)
        at, half = place(c, 1)
        pick, gates = picks(at, half)
        rows = ret[c].reshape(ROWS, 2 * W)
        high = gates.astype(BF16)
        low = (gates - high.astype(F32)).astype(BF16)
        tacc[half] += tn_dot(rows[:, 0:512], pick.astype(BF16))
        macc[half] += tn_dot(rows[:, 384:896], high) + tn_dot(rows[:, 384:896], low)

    loads[0].wait()
    loads[1].wait()
    pl.semaphore_wait(barrier, 19)

    def to_peer(src, dst, k):
        pltpu.make_async_remote_copy(
            src_ref=src,
            dst_ref=dst,
            send_sem=ps.at[k],
            recv_sem=pr.at[k],
            device_id=peer,
            device_id_type=MESH,
        ).start()

    def peer_wait(ref, sem):
        pltpu.make_async_copy(ref, ref, sem).wait()

    to_peer(rt_ref, rt2, 0)
    to_peer(gt_ref, gt2, 1)
    to_peer(tct.at[0], tct.at[1], 2)

    @pl.loop(0, AHEAD)
    def _(c):
        stage_pick(c)

    acc_in[...] = jnp.zeros_like(acc_in)
    acc_out[...] = jnp.zeros_like(acc_out)
    macc[...] = jnp.zeros_like(macc)
    tacc[...] = jnp.zeros_like(tacc)
    loads[2].wait()
    loads[3].wait()

    stages = (
        (stage_f, 5),
        (stage_e, 4),
        (stage_d, 3),
        (stage_c, 2),
        (stage_b, 1),
        (stage_a, 0),
        (stage_g, 6),
        (combine, LAG),
    )

    def guarded(stage, c):
        @pl.when(jnp.logical_and(c >= 0, c < NCH))
        def _():
            stage(c)

    @pl.loop(0, NCH + 6)
    def _(s):
        for stage, lag in stages:
            guarded(stage, s - lag)
            if lag == 0:

                @pl.when(s == 1)
                def _():
                    peer_wait(rt2, pr.at[0])
                    peer_wait(gt2, pr.at[1])
                    find_slots(1, rt2, gt2)
                    peer_wait(tct.at[1], pr.at[2])

                for k in range(2):
                    pick_at = AHEAD + 2 * (s - 1) + k
                    guarded(stage_pick, jnp.where(s > 0, pick_at, NCH))

        done = s - 5

        @pl.when(
            jnp.logical_and(
                jnp.logical_and(done >= BATCH, done < NCH), lax.rem(done, BATCH) == 0
            )
        )
        def _():
            stage_h(done - BATCH)

        @pl.when(s == LAST_1 + LAG)
        def _():
            pout[0:W, :] = tacc[1, 0:W, :].astype(BF16)
            pout[W : 2 * W, :] = macc[1, 64:512, :].astype(BF16)
            to_peer(pout, pin, 3)

    stage_h(NCH - BATCH)
    wig_ref[...] = acc_in[0:W, :].astype(BF16)
    wog_ref[...] = acc_out[64:512, :].astype(BF16)
    peer_wait(pin, pr.at[3])

    @pl.loop(NCH + 6 - LAG, NCH)
    def _(c):
        combine(c)

    tgrad_ref[...] = (tacc[0, 0:W, :] + pin[0:W, :].astype(F32)).astype(BF16)
    mixed_ref[...] = (macc[0, 64:512, :] + pin[W : 2 * W, :].astype(F32)).astype(BF16)
    peer_wait(rt2, ps.at[0])
    peer_wait(gt2, ps.at[1])
    peer_wait(pin, ps.at[2])
    peer_wait(pin, ps.at[3])

    def sent(ref, c, k):
        pltpu.make_async_copy(ref, ref, ss.at[c, k]).wait()

    @pl.loop(0, NCH)
    def _(c):
        @pl.when(local(c))
        def _():
            sent(x0.at[c, 0], c, 0)
            sent(outb.at[c, 0], c, 15)

        @pl.when(jnp.logical_not(local(c)))
        def _():
            sent(x0.at[c], c, 0)
            sent(outb.at[c], c, 15)

        for k in range(1, 15):
            sent(sx.at[c], c, k)
        for k in (16, 23):
            sent(rf.at[c], c, k)
        for k in range(17, 23):
            sent(q1.at[c], c, k)


def shards(tokens, routing, gate_weights, cotangent, w_in, w_out):
    vmem = pl.BlockSpec(memory_space=pltpu.VMEM)
    hbm = pl.BlockSpec(memory_space=pl.ANY)
    dma = pltpu.SemaphoreType.DMA
    mixed, tgrad, wig, wog = pl.pallas_call(
        kernel,
        name="experts",
        out_shape=(
            jax.ShapeDtypeStruct((W, TOK), BF16),
            jax.ShapeDtypeStruct((W, TOK), BF16),
            jax.ShapeDtypeStruct((W, 2 * H), BF16),
            jax.ShapeDtypeStruct((W, H), BF16),
        ),
        in_specs=[hbm, hbm, vmem, vmem, hbm, hbm],
        out_specs=(vmem, vmem, vmem, vmem),
        scratch_shapes=[
            pltpu.VMEM((2, 2 * W, TOK), BF16),
            pltpu.VMEM((512, 2 * H), BF16),
            pltpu.VMEM((512, H), BF16),
            pltpu.VMEM((2, 16, 2, TOK), F32),
            pltpu.VMEM((2, 16, 2, TOK), F32),
            pltpu.VMEM((NCH, 2, CAP, 2 * W), BF16),
            pltpu.VMEM((NCH, 2, CAP, 2 * W), BF16),
            pltpu.VMEM((NCH, 4, 2, RY, BW), BF16),
            pltpu.VMEM((NCH, 2, RY, BW), BF16),
            pltpu.VMEM((NCH, 4, RY, BW), BF16),
            pltpu.VMEM((NCH, RY, BW), BF16),
            pltpu.VMEM((NCH, RY, BW), BF16),
            pltpu.VMEM((NCH, 4, 2, RY, BW), BF16),
            pltpu.VMEM((NCH, 2, 4, RX, BW), BF16),
            pltpu.VMEM((NCH, 4, RX, BW), BF16),
            pltpu.VMEM((NCH, RX, BW), BF16),
            pltpu.VMEM((NCH, 2, RX, BW), BF16),
            pltpu.VMEM((NCH, 2, 4, RX, BW), BF16),
            pltpu.VMEM((NCH, 2, CAP, 2 * W), BF16),
            pltpu.VMEM((NCH, 2, CAP, 2 * W), BF16),
            pltpu.VMEM((2 * W, BATCH * ROWS), BF16),
            pltpu.VMEM((512, 2 * H), F32),
            pltpu.VMEM((512, H), F32),
            pltpu.VMEM((2, 512, TOK), F32),
            pltpu.VMEM((2, 512, TOK), F32),
            pltpu.VMEM((8, TOK), jnp.int32),
            pltpu.VMEM((8, TOK), F32),
            pltpu.VMEM((2 * W, TOK), BF16),
            pltpu.VMEM((2 * W, TOK), BF16),
            dma((4,)),
            dma((4,)),
            dma((4,)),
            dma((NCH, 24)),
            dma((NCH, 24)),
        ],
        compiler_params=pltpu.CompilerParams(
            collective_id=0, has_side_effects=True, vmem_limit_bytes=62 << 20
        ),
    )(tokens.T, cotangent.T, routing.T, gate_weights.T, w_in[0], w_out[0].T)
    return mixed.T, tgrad.T, wig[None], wog.T[None]


def solution(mesh):
    placed = (
        P("expert", ("pipe", "dp")),
        P("expert", None),
        P("expert", None),
        P("expert", ("pipe", "dp")),
        P("expert", ("pipe", "dp"), None),
        P("expert", None, ("pipe", "dp")),
    )
    return jax.shard_map(
        shards,
        mesh=mesh,
        in_specs=placed,
        out_specs=(
            P("expert", ("pipe", "dp")),
            P("expert", ("pipe", "dp")),
            P("expert", ("pipe", "dp"), None),
            P("expert", None, ("pipe", "dp")),
        ),
        check_vma=False,
    )
```

```python
import jax
import jax.numpy as jnp
from jax import lax
from jax.experimental import pallas as pl
from jax.experimental.pallas import tpu as pltpu
from jax.sharding import PartitionSpec as P

H = 1024
CAP = 48
TOK = 128
W = 448
NZ = 8
NCH = 16
ROWS = 2 * CAP
RY = 64
RX = 32
BW = 384
BATCH = 4
LAG = 7
ORDER = ((0, 0), (1, 0), (0, 1), (-1, 1), (2, 0), (3, 0), (-3, 0), (3, 1))
ORDER += ((-3, 1), (4, 0), (4, 1), (2, 1), (-2, 1), (1, 1), (-2, 0), (-1, 0))
LAST_1 = 13
LOCAL_1 = 2
RELAYS = ((1, 1, 0), (2, 1, 1), (3, 2, 0), (4, 2, 1), (5, 3, 0), (6, 3, 1), (8, 4, 0), (8, 4, 1))
MESH = pl.DeviceIdType.MESH
F32 = jnp.float32
BF16 = jnp.bfloat16


def nt_dot(a, b):
    return lax.dot_general(a, b, (((1,), (1,)), ((), ())), preferred_element_type=F32)


def tn_dot(a, b):
    return lax.dot_general(a, b, (((0,), (0,)), ((), ())), preferred_element_type=F32)


def dot(a, b):
    return jnp.dot(a, b, preferred_element_type=F32)


def kernel(
    tok_hbm,
    cot_hbm,
    rt_ref,
    gt_ref,
    win_hbm,
    wout_hbm,
    mixed_ref,
    tgrad_ref,
    wig_ref,
    wog_ref,
    ta,
    winp,
    woutp,
    code,
    gate,
    xr,
    sb,
    r1,
    r2,
    sx,
    rx,
    g,
    sb2,
    rf,
    q1,
    q2,
    g2,
    outb,
    ret,
    xt,
    acc_in,
    acc_out,
    macc,
    tacc,
    rg,
    rgs,
    pout,
    pin,
    w_sem,
    ps,
    pr,
    zs,
    zr,
    cs,
    cr,
    ts,
    tr,
    ss,
    rs,
):
    e, p, q = lax.axis_index("expert"), lax.axis_index("pipe"), lax.axis_index("dp")
    z, xhi, core = lax.div(e, 4), lax.rem(lax.div(e, 2), 2), lax.rem(e, 2)
    pu, pd, pf = lax.rem(p + 1, 4), lax.rem(p + 3, 4), lax.rem(p + 2, 4)
    up, dn, xp = (e, pu, q), (e, pd, q), (e, p, 1 - q)
    qo = 1 - q

    def send(src, dst, c, k, dev):
        pltpu.make_async_remote_copy(
            src_ref=src,
            dst_ref=dst,
            send_sem=ss.at[c, k],
            recv_sem=rs.at[c, k],
            device_id=dev,
            device_id_type=MESH,
        ).start()

    def wait(ref, c, k):
        pltpu.make_async_copy(ref, ref, rs.at[c, k]).wait()

    def place(c, sign):
        packed = jnp.int32(0)
        for i, (shift, half) in enumerate(ORDER):
            packed = jnp.where(c == i, 2 * (shift + NZ) + half, packed)
        shift, half = lax.div(packed, 2) - NZ, lax.rem(packed, 2)
        return 2 * lax.rem(z + sign * shift + NZ, NZ) + xhi, half, lax.rem(shift + NZ, NZ)

    barrier = pltpu.get_barrier_semaphore()
    peer = ((2 * z + 1 - xhi) * 2 + core, p, q)

    def greet(dev):
        pl.semaphore_signal(barrier, inc=1, device_id=dev, device_id_type=MESH)

    @pl.loop(0, 16)
    def _(d):
        other = (2 * lax.div(d, 2) + xhi) * 2 + lax.rem(d, 2)

        @pl.when(other != e)
        def _():
            greet((other, p, q))

    for dev in (up, dn, xp, peer):
        greet(dev)

    loads = [
        pltpu.make_async_copy(tok_hbm, ta.at[0, 0, core, pl.ds(0, W)], w_sem.at[0]),
        pltpu.make_async_copy(cot_hbm, ta.at[0, 0, core, pl.ds(W, W)], w_sem.at[1]),
        pltpu.make_async_copy(win_hbm, winp.at[pl.ds(0, W)], w_sem.at[2]),
        pltpu.make_async_copy(wout_hbm, woutp.at[pl.ds(64, W)], w_sem.at[3]),
    ]
    for load in loads:
        load.start()
    winp[pl.ds(W, 64), :] = jnp.zeros((64, 2 * H), BF16)
    woutp[pl.ds(0, 64), :] = jnp.zeros((64, H), BF16)

    ids = lax.broadcasted_iota(jnp.int32, (32, TOK), 0).astype(F32)
    mine_id = e.astype(F32)
    before = jnp.where(
        lax.broadcasted_iota(jnp.int32, (TOK, TOK), 0)
        < lax.broadcasted_iota(jnp.int32, (TOK, TOK), 1),
        1.0,
        0.0,
    ).astype(BF16)

    def find_slots(half):
        rt, gt = rg[half, 0:8, :], rg[half, 8:16, :]
        hit = jnp.zeros((32, TOK), F32)
        weight = jnp.zeros((32, TOK), F32)
        for k in range(8):
            same = rt[k : k + 1, :] == ids
            hit = hit + jnp.where(same, 1.0, 0.0)
            weight = weight + jnp.where(same, gt[k : k + 1, :], 0.0)
        marked = jnp.where(hit > 0.5, dot(hit.astype(BF16), before), -1.0)
        for i in range(16):
            code[half, i, :, :] = marked[2 * i : 2 * i + 2, :]
            gate[half, i, :, :] = weight[2 * i : 2 * i + 2, :]

    rg[0, 0:8, :] = rt_ref[...].astype(F32)
    rg[0, 8:16, :] = gt_ref[...]

    row_ids = lax.broadcasted_iota(jnp.int32, (CAP, TOK), 0).astype(F32)
    lanes = lax.broadcasted_iota(jnp.int32, (CAP, 2 * W), 1)

    def picks(at, half):
        cq, gq = code[half, at], gate[half, at]
        chosen = [cq[j : j + 1, :] == row_ids for j in range(2)]
        pick = [jnp.where(m, 1.0, 0.0) for m in chosen]
        gates = [jnp.where(m, gq[j : j + 1, :], 0.0) for j, m in enumerate(chosen)]
        return jnp.concatenate(pick, axis=0), jnp.concatenate(gates, axis=0)

    def local(c):
        return jnp.logical_or(c == 0, c == LOCAL_1)

    def deliver(src, dst, c, k, at):
        for j in range(2):
            own = jnp.logical_and(local(c), core == j)

            @pl.when(own)
            def _():
                pltpu.make_async_copy(src.at[c, j], dst.at[c, core], rs.at[c, k]).start()

            @pl.when(jnp.logical_not(own))
            def _():
                send(src.at[c, j], dst.at[c, core], c, k, (at * 2 + j, p, q))

    def stage_pick(c):
        _, half, o = place(c, 1)
        hold(rgs.at[o, half], tr.at[o, half])
        hold(ta.at[o, half, 1 - core], cr.at[o, half])
        for k in range(2):
            same = rgs[o, half, k, 0:8, :] == mine_id
            hit = jnp.sum(jnp.where(same, 1.0, 0.0), axis=0, keepdims=True)
            gates = jnp.where(same, rgs[o, half, k, 8:16, :], 0.0)
            gates = jnp.sum(gates, axis=0, keepdims=True)
            many = jnp.broadcast_to(hit, (16, TOK)).astype(BF16)
            mark = jnp.where(hit > 0.5, dot(many, before)[0:1, :], -1.0)
            chosen = mark == row_ids
            row_gate = jnp.sum(jnp.where(chosen, gates, 0.0), axis=1, keepdims=True)
            pick = jnp.where(chosen, 1.0, 0.0).astype(BF16)
            rows = nt_dot(pick, ta[o, half, k])
            rows = jnp.where(lanes >= W, rows * row_gate, rows)
            xr[c, k] = rows.astype(BF16)

    def stage_a(c):
        stage_pick(c)
        rows = xr[c].reshape(ROWS, 2 * W)
        x, dy = rows[:, 0:512], rows[:, 384:896]
        for k, pp in enumerate((pf, pu, pd, p)):
            at = pl.multiple_of(pp * 256, 256)
            gp = dot(x, winp[:, pl.ds(at, 256)]).astype(BF16)
            un = dot(x, winp[:, pl.ds(at + H, 256)]).astype(BF16)
            bk = dot(dy, woutp[:, pl.ds(at, 256)]).astype(BF16)
            for h in range(2):
                s = slice(h * 128, h * 128 + 128)
                for i, v in enumerate((gp, un, bk)):
                    t = slice(i * 128, i * 128 + 128)
                    sb[c, pp, h, :, t] = v[0:RY, s]
                    sb2[c, h, pp, :, t] = v[RY:ROWS, s]
            if k == 0:
                send(sb.at[c, pf, 0], r1.at[c, 0], c, 1, up)
                send(sb.at[c, pf, 1], r1.at[c, 1], c, 2, dn)
            if k == 1:
                send(sb.at[c, pu, 1], r2.at[c, 0], c, 3, up)
            if k == 2:
                send(sb.at[c, pd, 0], r2.at[c, 1], c, 4, dn)
        send(sb2.at[c, qo], rf.at[c], c, 16, xp)

    def by_parity(c, run):
        @pl.when(lax.rem(c, 2) == 0)
        def _():
            run(up, pu, dn, pd)

        @pl.when(lax.rem(c, 2) == 1)
        def _():
            run(dn, pd, up, pu)

    def stage_b(c):
        wait(r1.at[c, 0], c, 1)
        sb[c, pu, 0] = (sb[c, pu, 0].astype(F32) + r1[c, 0].astype(F32)).astype(BF16)
        send(sb.at[c, pu, 0], r2.at[c, 2], c, 5, up)
        wait(r1.at[c, 1], c, 2)
        sb[c, pd, 1] = (sb[c, pd, 1].astype(F32) + r1[c, 1].astype(F32)).astype(BF16)
        send(sb.at[c, pd, 1], r2.at[c, 3], c, 6, dn)
        wait(rf.at[c], c, 16)
        sb2[c, q] = (sb2[c, q].astype(F32) + rf[c].astype(F32)).astype(BF16)

        def run(a, pa, b, pb):
            send(sb2.at[c, q, pf], q1.at[c], c, 17, a)
            send(sb2.at[c, q, pb], q2.at[c, 1], c, 18, b)

        by_parity(c, run)

    def y_sum(c, h):
        return (
            sb[c, p, h].astype(F32)
            + r2[c, 1 - h].astype(F32)
            + r2[c, 2 + h].astype(F32)
        )

    def stage_c(c):
        for k in range(4):
            wait(r2.at[c, k], c, 3 + k)
        sx[c] = y_sum(c, qo).astype(BF16)
        send(sx.at[c], rx.at[c], c, 7, xp)
        wait(q1.at[c], c, 17)

        def run(a, pa, b, pb):
            sb2[c, q, pa] = (sb2[c, q, pa].astype(F32) + q1[c].astype(F32)).astype(BF16)
            send(sb2.at[c, q, pa], q2.at[c, 0], c, 19, a)

        by_parity(c, run)

    def activate(total):
        gp, un, bk = total[:, 0:128], total[:, 128:256], total[:, 256:384]
        s = 1.0 / (1.0 + jnp.exp(-gp))
        act = gp * s
        return jnp.concatenate(
            [act * un, bk * un * (s * (1.0 + gp * (1.0 - s))), bk * act], axis=1
        ).astype(BF16)

    def stage_d(c):
        wait(rx.at[c], c, 7)
        g[c, p, q] = activate(y_sum(c, q) + rx[c].astype(F32))
        mine = g.at[c, p, q]
        send(mine, mine, c, 8, xp)
        send(mine, mine, c, 9, up)
        send(mine, mine, c, 10, dn)
        wait(q2.at[c, 1], c, 18)
        wait(q2.at[c, 0], c, 19)
        g2[c, q, p] = activate(
            sb2[c, q, p].astype(F32) + q2[c, 0].astype(F32) + q2[c, 1].astype(F32)
        )
        mine2 = g2.at[c, q, p]
        send(mine2, mine2, c, 20, up)
        send(mine2, mine2, c, 21, dn)

    def stage_e(c):
        other = g.at[c, p, qo]
        wait(other, c, 8)
        send(other, other, c, 11, up)
        send(other, other, c, 12, dn)
        wait(g2.at[c, q, pd], c, 20)
        wait(g2.at[c, q, pu], c, 21)

        def run(a, pa, b, pb):
            send(g2.at[c, q, pb], g2.at[c, q, pb], c, 22, a)

        by_parity(c, run)

    def stage_f(c):
        wait(g.at[c, pd, q], c, 9)
        wait(g.at[c, pu, q], c, 10)
        wait(g.at[c, pd, qo], c, 11)
        wait(g.at[c, pu, qo], c, 12)
        send(g.at[c, pd, 0], g.at[c, pd, 0], c, 13, up)
        send(g.at[c, pu, 1], g.at[c, pu, 1], c, 14, dn)
        wait(g2.at[c, q, pf], c, 22)
        send(g2.at[c, q], g2.at[c, q], c, 23, xp)

    def stage_g(c):
        wait(g.at[c, pf, 0], c, 13)
        wait(g.at[c, pf, 1], c, 14)
        wait(g2.at[c, qo], c, 23)

        def part(k):
            s = slice(k * 128, k * 128 + 128)
            y = [g[c, i // 2, i % 2, :, s] for i in range(8)]
            x = [g2[c, i % 2, i // 2, :, s] for i in range(8)]
            return jnp.concatenate(
                [jnp.concatenate(y, axis=1), jnp.concatenate(x, axis=1)], axis=0
            )

        back = nt_dot(part(1), winp[:, 0:H]) + nt_dot(part(2), winp[:, H : 2 * H])
        out = nt_dot(part(0), woutp[...])
        for j in range(2):
            s = slice(j * CAP, j * CAP + CAP)
            outb[c, j, :, 0:384] = back[s, 0:384].astype(BF16)
            outb[c, j, :, 384:512] = (back[s, 384:512] + out[s, 0:128]).astype(BF16)
            outb[c, j, :, 512:896] = out[s, 128:512].astype(BF16)
        deliver(outb, ret, c, 15, place(c, -1)[0])

    def stage_h(first):
        rows = xr[pl.ds(first, BATCH)].reshape(BATCH * ROWS, 2 * W)
        xt[...] = rows.T

        @pl.loop(0, 4)
        def _(pp):
            def pair(k):
                s = slice(k * 128, k * 128 + 128)
                parts = []
                for b in range(BATCH):
                    c = first + b
                    y = [g[c, pp, h, :, s] for h in range(2)]
                    x = [g2[c, h, pp, :, s] for h in range(2)]
                    parts += [jnp.concatenate(y, axis=1), jnp.concatenate(x, axis=1)]
                return jnp.concatenate(parts, axis=0)

            at = pl.multiple_of(pp * 256, 256)
            acc_in[:, pl.ds(at, 256)] += dot(xt[0:512, :], pair(1))
            acc_in[:, pl.ds(at + H, 256)] += dot(xt[0:512, :], pair(2))
            acc_out[:, pl.ds(at, 256)] += dot(xt[384:896, :], pair(0))

    def combine(c):
        wait(ret.at[c], c, 15)
        at, half, _ = place(c, 1)
        pick, gates = picks(at, half)
        rows = ret[c].reshape(ROWS, 2 * W)
        high = gates.astype(BF16)
        low = (gates - high.astype(F32)).astype(BF16)
        tacc[half] += tn_dot(rows[:, 0:512], pick.astype(BF16))
        macc[half] += tn_dot(rows[:, 384:896], high) + tn_dot(rows[:, 384:896], low)

    def push(src, dst, ssem, rsem, dev):
        pltpu.make_async_remote_copy(
            src_ref=src,
            dst_ref=dst,
            send_sem=ssem,
            recv_sem=rsem,
            device_id=dev,
            device_id_type=MESH,
        ).start()

    def hold(ref, sem):
        pltpu.make_async_copy(ref, ref, sem).wait()

    zu = ((2 * lax.rem(z + 1, NZ) + xhi) * 2 + core, p, q)
    zd = ((2 * lax.rem(z + NZ - 1, NZ) + xhi) * 2 + core, p, q)
    twin = ((2 * z + xhi) * 2 + 1 - core, p, q)

    def onward(o, half, dst, dev):
        push(
            ta.at[o, half, core],
            ta.at[dst, half, core],
            zs.at[dst, half],
            zr.at[dst, half],
            dev,
        )

    def share(o, half):
        block = ta.at[o, half, core]
        push(block, block, cs.at[o, half], cr.at[o, half], twin)

    def tables(half):
        @pl.loop(0, 16)
        def _(d):
            zz, k = lax.div(d, 2), lax.rem(d, 2)
            other = (2 * zz + xhi) * 2 + k
            o = lax.rem(zz - z + NZ, NZ)
            dst = rgs.at[o, half, core]

            @pl.when(other != e)
            def _():
                push(rg.at[half], dst, ts.at[half, d], tr.at[o, half], (other, p, q))

            @pl.when(other == e)
            def _():
                pltpu.make_async_copy(rg.at[half], dst, tr.at[o, half]).start()

    loads[0].wait()
    loads[1].wait()
    pl.semaphore_wait(barrier, 19)
    push(rg.at[0], rg.at[1], ps.at[0], pr.at[0], peer)
    tables(0)
    share(0, 0)
    push(ta.at[0, 0, core], ta.at[0, 1, core], ps.at[1], pr.at[1], peer)
    onward(0, 0, 1, zu)
    onward(0, 0, 7, zd)
    find_slots(0)

    acc_in[...] = jnp.zeros_like(acc_in)
    acc_out[...] = jnp.zeros_like(acc_out)
    macc[...] = jnp.zeros_like(macc)
    tacc[...] = jnp.zeros_like(tacc)
    loads[2].wait()
    loads[3].wait()

    stages = (
        (stage_f, 5),
        (stage_e, 4),
        (stage_d, 3),
        (stage_c, 2),
        (stage_b, 1),
        (stage_a, 0),
        (stage_g, 6),
        (combine, LAG),
    )

    def guarded(stage, c):
        @pl.when(jnp.logical_and(c >= 0, c < NCH))
        def _():
            stage(c)

    @pl.loop(0, NCH + 6)
    def _(s):
        for stage, lag in stages:
            guarded(stage, s - lag)
            if lag == 0:

                @pl.when(s == 0)
                def _():
                    hold(rg.at[1], pr.at[0])
                    tables(1)
                    find_slots(1)
                    hold(ta.at[0, 1, core], pr.at[1])
                    onward(0, 1, 1, zu)
                    onward(0, 1, 7, zd)
                    share(0, 1)

        for at, far, half in RELAYS:

            @pl.when(s == at - 1)
            def _():
                if far < 4 or half == 0:
                    hold(ta.at[far, half, core], zr.at[far, half])
                    if far < 3 or (far == 3 and half == 0):
                        onward(far, half, far + 1, zu)
                    share(far, half)
                if far < 4 or half == 1:
                    back = NZ - far
                    hold(ta.at[back, half, core], zr.at[back, half])
                    if far < 3 or (far == 3 and half == 1):
                        onward(back, half, back - 1, zd)
                    share(back, half)

        done = s - 5

        @pl.when(
            jnp.logical_and(
                jnp.logical_and(done >= BATCH, done < NCH), lax.rem(done, BATCH) == 0
            )
        )
        def _():
            stage_h(done - BATCH)

        @pl.when(s == LAST_1 + LAG)
        def _():
            pout[0:W, :] = tacc[1, 0:W, :].astype(BF16)
            pout[W : 2 * W, :] = macc[1, 64:512, :].astype(BF16)
            push(pout, pin, ps.at[2], pr.at[2], peer)

    stage_h(NCH - BATCH)
    wig_ref[...] = acc_in[0:W, :].astype(BF16)
    wog_ref[...] = acc_out[64:512, :].astype(BF16)
    hold(pin, pr.at[2])

    @pl.loop(NCH + 6 - LAG, NCH)
    def _(c):
        combine(c)

    tgrad_ref[...] = (tacc[0, 0:W, :] + pin[0:W, :].astype(F32)).astype(BF16)
    mixed_ref[...] = (macc[0, 64:512, :] + pin[W : 2 * W, :].astype(F32)).astype(BF16)
    hold(rg.at[1], ps.at[0])
    hold(pin, ps.at[1])
    hold(pin, ps.at[2])

    @pl.loop(0, 2)
    def _(half):
        @pl.loop(0, 16)
        def _(d):
            @pl.when((2 * lax.div(d, 2) + xhi) * 2 + lax.rem(d, 2) != e)
            def _():
                hold(rg.at[half], ts.at[half, d])

        @pl.loop(0, NZ)
        def _(o):
            hold(pin, cs.at[o, half])

            @pl.when(o > 0)
            def _():
                hold(pin, zs.at[o, half])

    def sent(ref, c, k):
        pltpu.make_async_copy(ref, ref, ss.at[c, k]).wait()

    @pl.loop(0, NCH)
    def _(c):
        @pl.when(local(c))
        def _():
            sent(outb.at[c, 0], c, 15)

        @pl.when(jnp.logical_not(local(c)))
        def _():
            sent(outb.at[c], c, 15)

        for k in range(1, 15):
            sent(sx.at[c], c, k)
        for k in (16, 23):
            sent(rf.at[c], c, k)
        for k in range(17, 23):
            sent(q1.at[c], c, k)


def shards(tokens, routing, gate_weights, cotangent, w_in, w_out):
    vmem = pl.BlockSpec(memory_space=pltpu.VMEM)
    hbm = pl.BlockSpec(memory_space=pl.ANY)
    dma = pltpu.SemaphoreType.DMA
    mixed, tgrad, wig, wog = pl.pallas_call(
        kernel,
        name="experts",
        out_shape=(
            pltpu.VMEM((W, TOK), BF16),
            pltpu.VMEM((W, TOK), BF16),
            pltpu.VMEM((W, 2 * H), BF16),
            pltpu.VMEM((W, H), BF16),
        ),
        in_specs=[hbm, hbm, vmem, vmem, hbm, hbm],
        out_specs=(vmem, vmem, vmem, vmem),
        scratch_shapes=[
            pltpu.VMEM((NZ, 2, 2, 2 * W, TOK), BF16),
            pltpu.VMEM((512, 2 * H), BF16),
            pltpu.VMEM((512, H), BF16),
            pltpu.VMEM((2, 16, 2, TOK), F32),
            pltpu.VMEM((2, 16, 2, TOK), F32),
            pltpu.VMEM((NCH, 2, CAP, 2 * W), BF16),
            pltpu.VMEM((NCH, 4, 2, RY, BW), BF16),
            pltpu.VMEM((NCH, 2, RY, BW), BF16),
            pltpu.VMEM((NCH, 4, RY, BW), BF16),
            pltpu.VMEM((NCH, RY, BW), BF16),
            pltpu.VMEM((NCH, RY, BW), BF16),
            pltpu.VMEM((NCH, 4, 2, RY, BW), BF16),
            pltpu.VMEM((NCH, 2, 4, RX, BW), BF16),
            pltpu.VMEM((NCH, 4, RX, BW), BF16),
            pltpu.VMEM((NCH, RX, BW), BF16),
            pltpu.VMEM((NCH, 2, RX, BW), BF16),
            pltpu.VMEM((NCH, 2, 4, RX, BW), BF16),
            pltpu.VMEM((NCH, 2, CAP, 2 * W), BF16),
            pltpu.VMEM((NCH, 2, CAP, 2 * W), BF16),
            pltpu.VMEM((2 * W, BATCH * ROWS), BF16),
            pltpu.VMEM((512, 2 * H), F32),
            pltpu.VMEM((512, H), F32),
            pltpu.VMEM((2, 512, TOK), F32),
            pltpu.VMEM((2, 512, TOK), F32),
            pltpu.VMEM((2, 16, TOK), F32),
            pltpu.VMEM((NZ, 2, 2, 16, TOK), F32),
            pltpu.VMEM((2 * W, TOK), BF16),
            pltpu.VMEM((2 * W, TOK), BF16),
            dma((4,)),
            dma((3,)),
            dma((3,)),
            dma((NZ, 2)),
            dma((NZ, 2)),
            dma((NZ, 2)),
            dma((NZ, 2)),
            dma((2, 16)),
            dma((NZ, 2)),
            dma((NCH, 24)),
            dma((NCH, 24)),
        ],
        compiler_params=pltpu.CompilerParams(
            collective_id=0, has_side_effects=True, vmem_limit_bytes=57 << 20
        ),
    )(tokens.T, cotangent.T, routing.T, gate_weights.T, w_in[0], w_out[0].T)
    return mixed.T, tgrad.T, wig[None], wog.T[None]


def solution(mesh):
    placed = (
        P("expert", ("pipe", "dp")),
        P("expert", None),
        P("expert", None),
        P("expert", ("pipe", "dp")),
        P("expert", ("pipe", "dp"), None),
        P("expert", None, ("pipe", "dp")),
    )
    return jax.shard_map(
        shards,
        mesh=mesh,
        in_specs=placed,
        out_specs=(
            P("expert", ("pipe", "dp")),
            P("expert", ("pipe", "dp")),
            P("expert", ("pipe", "dp"), None),
            P("expert", None, ("pipe", "dp")),
        ),
        check_vma=False,
    )
```

```python
import jax
import jax.numpy as jnp
from jax import lax
from jax.experimental import pallas as pl
from jax.experimental.pallas import tpu as pltpu
from jax.sharding import PartitionSpec as P

H = 1024
CAP = 48
TOK = 128
W = 448
NZ = 8
NCH = 16
ROWS = 2 * CAP
RY = 64
RX = 32
BW = 384
AHEAD = 3
BATCH = 4
LAG = 10
ORDER = ((0, 0), (2, 0), (-2, 0), (0, 1), (1, 1), (-1, 1), (2, 1), (-2, 1))
ORDER += ((4, 1), (4, 0), (3, 1), (-3, 1), (3, 0), (-3, 0), (1, 0), (-1, 0))
LAST_1 = 11
LOCAL_1 = 3
MESH = pl.DeviceIdType.MESH
F32 = jnp.float32
BF16 = jnp.bfloat16


def nt_dot(a, b):
    return lax.dot_general(a, b, (((1,), (1,)), ((), ())), preferred_element_type=F32)


def tn_dot(a, b):
    return lax.dot_general(a, b, (((0,), (0,)), ((), ())), preferred_element_type=F32)


def dot(a, b):
    return jnp.dot(a, b, preferred_element_type=F32)


def kernel(
    tok_hbm,
    cot_hbm,
    rt_ref,
    gt_ref,
    win_hbm,
    wout_hbm,
    mixed_ref,
    tgrad_ref,
    wig_ref,
    wog_ref,
    tct,
    winp,
    woutp,
    code,
    gate,
    x0,
    xr,
    sb,
    r1,
    r2,
    sx,
    rx,
    g,
    sb2,
    rf,
    q1,
    q2,
    g2,
    outb,
    ret,
    xt,
    acc_in,
    acc_out,
    macc,
    tacc,
    rt2,
    gt2,
    pout,
    pin,
    w_sem,
    ps,
    pr,
    ss,
    rs,
):
    e, p, q = lax.axis_index("expert"), lax.axis_index("pipe"), lax.axis_index("dp")
    z, xhi, core = lax.div(e, 4), lax.rem(lax.div(e, 2), 2), lax.rem(e, 2)
    pu, pd, pf = lax.rem(p + 1, 4), lax.rem(p + 3, 4), lax.rem(p + 2, 4)
    up, dn, xp = (e, pu, q), (e, pd, q), (e, p, 1 - q)
    qo = 1 - q

    def send(src, dst, c, k, dev):
        pltpu.make_async_remote_copy(
            src_ref=src,
            dst_ref=dst,
            send_sem=ss.at[c, k],
            recv_sem=rs.at[c, k],
            device_id=dev,
            device_id_type=MESH,
        ).start()

    def wait(ref, c, k):
        pltpu.make_async_copy(ref, ref, rs.at[c, k]).wait()

    def place(c, sign):
        packed = jnp.int32(0)
        for i, (shift, half) in enumerate(ORDER):
            packed = jnp.where(c == i, 2 * (shift + NZ) + half, packed)
        shift, half = lax.div(packed, 2) - NZ, lax.rem(packed, 2)
        return 2 * lax.rem(z + sign * shift + NZ, NZ) + xhi, half

    barrier = pltpu.get_barrier_semaphore()
    peer = ((2 * z + 1 - xhi) * 2 + core, p, q)

    def greet(dev):
        pl.semaphore_signal(barrier, inc=1, device_id=dev, device_id_type=MESH)

    @pl.loop(0, 16)
    def _(d):
        other = (2 * lax.div(d, 2) + xhi) * 2 + lax.rem(d, 2)

        @pl.when(other != e)
        def _():
            greet((other, p, q))

    for dev in (up, dn, xp, peer):
        greet(dev)

    loads = [
        pltpu.make_async_copy(tok_hbm, tct.at[0, pl.ds(0, W)], w_sem.at[0]),
        pltpu.make_async_copy(cot_hbm, tct.at[0, pl.ds(W, W)], w_sem.at[1]),
        pltpu.make_async_copy(win_hbm, winp.at[pl.ds(0, W)], w_sem.at[2]),
        pltpu.make_async_copy(wout_hbm, woutp.at[pl.ds(64, W)], w_sem.at[3]),
    ]
    for load in loads:
        load.start()
    winp[pl.ds(W, 64), :] = jnp.zeros((64, 2 * H), BF16)
    woutp[pl.ds(0, 64), :] = jnp.zeros((64, H), BF16)

    ids = lax.broadcasted_iota(jnp.int32, (32, TOK), 0)
    before = jnp.where(
        lax.broadcasted_iota(jnp.int32, (TOK, TOK), 0)
        < lax.broadcasted_iota(jnp.int32, (TOK, TOK), 1),
        1.0,
        0.0,
    ).astype(BF16)

    def find_slots(half, rt, gt):
        hit = jnp.zeros((32, TOK), F32)
        weight = jnp.zeros((32, TOK), F32)
        for k in range(8):
            same = rt[k : k + 1, :] == ids
            hit = hit + jnp.where(same, 1.0, 0.0)
            weight = weight + jnp.where(same, gt[k : k + 1, :], 0.0)
        marked = jnp.where(hit > 0.5, dot(hit.astype(BF16), before), -1.0)
        for i in range(16):
            code[half, i, :, :] = marked[2 * i : 2 * i + 2, :]
            gate[half, i, :, :] = weight[2 * i : 2 * i + 2, :]

    find_slots(0, rt_ref, gt_ref)

    row_ids = lax.broadcasted_iota(jnp.int32, (CAP, TOK), 0).astype(F32)
    lanes = lax.broadcasted_iota(jnp.int32, (ROWS, 2 * W), 1)

    def picks(at, half):
        cq, gq = code[half, at], gate[half, at]
        chosen = [cq[j : j + 1, :] == row_ids for j in range(2)]
        pick = [jnp.where(m, 1.0, 0.0) for m in chosen]
        gates = [jnp.where(m, gq[j : j + 1, :], 0.0) for j, m in enumerate(chosen)]
        return jnp.concatenate(pick, axis=0), jnp.concatenate(gates, axis=0)

    def local(c):
        return jnp.logical_or(c == 0, c == LOCAL_1)

    def deliver(src, dst, c, k, at):
        for j in range(2):
            own = jnp.logical_and(local(c), core == j)

            @pl.when(own)
            def _():
                pltpu.make_async_copy(src.at[c, j], dst.at[c, core], rs.at[c, k]).start()

            @pl.when(jnp.logical_not(own))
            def _():
                send(src.at[c, j], dst.at[c, core], c, k, (at * 2 + j, p, q))

    def stage_pick(c):
        at, half = place(c, 1)
        pick, gates = picks(at, half)
        row_gate = jnp.sum(gates, axis=1, keepdims=True)
        rows = nt_dot(pick.astype(BF16), tct[half])
        rows = jnp.where(lanes >= W, rows * row_gate, rows).astype(BF16)
        x0[c] = rows.reshape(2, CAP, 2 * W)
        deliver(x0, xr, c, 0, at)

    def stage_a(c):
        wait(xr.at[c], c, 0)
        rows = xr[c].reshape(ROWS, 2 * W)
        x, dy = rows[:, 0:512], rows[:, 384:896]
        for k, pp in enumerate((pf, pu, pd, p)):
            at = pl.multiple_of(pp * 256, 256)
            gp = dot(x, winp[:, pl.ds(at, 256)]).astype(BF16)
            un = dot(x, winp[:, pl.ds(at + H, 256)]).astype(BF16)
            bk = dot(dy, woutp[:, pl.ds(at, 256)]).astype(BF16)
            for h in range(2):
                s = slice(h * 128, h * 128 + 128)
                for i, v in enumerate((gp, un, bk)):
                    t = slice(i * 128, i * 128 + 128)
                    sb[c, pp, h, :, t] = v[0:RY, s]
                    sb2[c, h, pp, :, t] = v[RY:ROWS, s]
            if k == 0:
                send(sb.at[c, pf, 0], r1.at[c, 0], c, 1, up)
                send(sb.at[c, pf, 1], r1.at[c, 1], c, 2, dn)
            if k == 1:
                send(sb.at[c, pu, 1], r2.at[c, 0], c, 3, up)
            if k == 2:
                send(sb.at[c, pd, 0], r2.at[c, 1], c, 4, dn)
        send(sb2.at[c, qo], rf.at[c], c, 16, xp)

    def by_parity(c, run):
        @pl.when(lax.rem(c, 2) == 0)
        def _():
            run(up, pu, dn, pd)

        @pl.when(lax.rem(c, 2) == 1)
        def _():
            run(dn, pd, up, pu)

    def stage_b(c):
        wait(r1.at[c, 0], c, 1)
        sb[c, pu, 0] = (sb[c, pu, 0].astype(F32) + r1[c, 0].astype(F32)).astype(BF16)
        send(sb.at[c, pu, 0], r2.at[c, 2], c, 5, up)
        wait(r1.at[c, 1], c, 2)
        sb[c, pd, 1] = (sb[c, pd, 1].astype(F32) + r1[c, 1].astype(F32)).astype(BF16)
        send(sb.at[c, pd, 1], r2.at[c, 3], c, 6, dn)
        wait(rf.at[c], c, 16)
        sb2[c, q] = (sb2[c, q].astype(F32) + rf[c].astype(F32)).astype(BF16)

        def run(a, pa, b, pb):
            send(sb2.at[c, q, pf], q1.at[c], c, 17, a)
            send(sb2.at[c, q, pb], q2.at[c, 1], c, 18, b)

        by_parity(c, run)

    def y_sum(c, h):
        return (
            sb[c, p, h].astype(F32)
            + r2[c, 1 - h].astype(F32)
            + r2[c, 2 + h].astype(F32)
        )

    def stage_c(c):
        for k in range(4):
            wait(r2.at[c, k], c, 3 + k)
        sx[c] = y_sum(c, qo).astype(BF16)
        send(sx.at[c], rx.at[c], c, 7, xp)
        wait(q1.at[c], c, 17)

        def run(a, pa, b, pb):
            sb2[c, q, pa] = (sb2[c, q, pa].astype(F32) + q1[c].astype(F32)).astype(BF16)
            send(sb2.at[c, q, pa], q2.at[c, 0], c, 19, a)

        by_parity(c, run)

    def activate(total):
        gp, un, bk = total[:, 0:128], total[:, 128:256], total[:, 256:384]
        s = 1.0 / (1.0 + jnp.exp(-gp))
        act = gp * s
        return jnp.concatenate(
            [act * un, bk * un * (s * (1.0 + gp * (1.0 - s))), bk * act], axis=1
        ).astype(BF16)

    def stage_d(c):
        wait(rx.at[c], c, 7)
        g[c, p, q] = activate(y_sum(c, q) + rx[c].astype(F32))
        mine = g.at[c, p, q]
        send(mine, mine, c, 8, xp)
        send(mine, mine, c, 9, up)
        send(mine, mine, c, 10, dn)
        wait(q2.at[c, 1], c, 18)
        wait(q2.at[c, 0], c, 19)
        g2[c, q, p] = activate(
            sb2[c, q, p].astype(F32) + q2[c, 0].astype(F32) + q2[c, 1].astype(F32)
        )
        mine2 = g2.at[c, q, p]
        send(mine2, mine2, c, 20, up)
        send(mine2, mine2, c, 21, dn)

    def stage_e(c):
        other = g.at[c, p, qo]
        wait(other, c, 8)
        send(other, other, c, 11, up)
        send(other, other, c, 12, dn)
        wait(g2.at[c, q, pd], c, 20)
        wait(g2.at[c, q, pu], c, 21)

        def run(a, pa, b, pb):
            send(g2.at[c, q, pb], g2.at[c, q, pb], c, 22, a)

        by_parity(c, run)

    def stage_f(c):
        wait(g.at[c, pd, q], c, 9)
        wait(g.at[c, pu, q], c, 10)
        wait(g.at[c, pd, qo], c, 11)
        wait(g.at[c, pu, qo], c, 12)
        send(g.at[c, pd, 0], g.at[c, pd, 0], c, 13, up)
        send(g.at[c, pu, 1], g.at[c, pu, 1], c, 14, dn)
        wait(g2.at[c, q, pf], c, 22)
        send(g2.at[c, q], g2.at[c, q], c, 23, xp)

    def stage_g(c):
        wait(g.at[c, pf, 0], c, 13)
        wait(g.at[c, pf, 1], c, 14)
        wait(g2.at[c, qo], c, 23)

        def part(k):
            s = slice(k * 128, k * 128 + 128)
            y = [g[c, i // 2, i % 2, :, s] for i in range(8)]
            x = [g2[c, i % 2, i // 2, :, s] for i in range(8)]
            return jnp.concatenate(
                [jnp.concatenate(y, axis=1), jnp.concatenate(x, axis=1)], axis=0
            )

        back = nt_dot(part(1), winp[:, 0:H]) + nt_dot(part(2), winp[:, H : 2 * H])
        out = nt_dot(part(0), woutp[...])
        for j in range(2):
            s = slice(j * CAP, j * CAP + CAP)
            outb[c, j, :, 0:384] = back[s, 0:384].astype(BF16)
            outb[c, j, :, 384:512] = (back[s, 384:512] + out[s, 0:128]).astype(BF16)
            outb[c, j, :, 512:896] = out[s, 128:512].astype(BF16)
        deliver(outb, ret, c, 15, place(c, -1)[0])

    def stage_h(first):
        rows = xr[pl.ds(first, BATCH)].reshape(BATCH * ROWS, 2 * W)
        xt[...] = rows.T

        @pl.loop(0, 4)
        def _(pp):
            def pair(k):
                s = slice(k * 128, k * 128 + 128)
                parts = []
                for b in range(BATCH):
                    c = first + b
                    y = [g[c, pp, h, :, s] for h in range(2)]
                    x = [g2[c, h, pp, :, s] for h in range(2)]
                    parts += [jnp.concatenate(y, axis=1), jnp.concatenate(x, axis=1)]
                return jnp.concatenate(parts, axis=0)

            at = pl.multiple_of(pp * 256, 256)
            acc_in[:, pl.ds(at, 256)] += dot(xt[0:512, :], pair(1))
            acc_in[:, pl.ds(at + H, 256)] += dot(xt[0:512, :], pair(2))
            acc_out[:, pl.ds(at, 256)] += dot(xt[384:896, :], pair(0))

    def combine(c):
        wait(ret.at[c], c, 15)
        at, half = place(c, 1)
        pick, gates = picks(at, half)
        rows = ret[c].reshape(ROWS, 2 * W)
        high = gates.astype(BF16)
        low = (gates - high.astype(F32)).astype(BF16)
        tacc[half] += tn_dot(rows[:, 0:512], pick.astype(BF16))
        macc[half] += tn_dot(rows[:, 384:896], high) + tn_dot(rows[:, 384:896], low)

    loads[0].wait()
    loads[1].wait()
    pl.semaphore_wait(barrier, 19)

    def to_peer(src, dst, k):
        pltpu.make_async_remote_copy(
            src_ref=src,
            dst_ref=dst,
            send_sem=ps.at[k],
            recv_sem=pr.at[k],
            device_id=peer,
            device_id_type=MESH,
        ).start()

    def peer_wait(ref, sem):
        pltpu.make_async_copy(ref, ref, sem).wait()

    to_peer(rt_ref, rt2, 0)
    to_peer(gt_ref, gt2, 1)
    to_peer(tct.at[0], tct.at[1], 2)

    @pl.loop(0, AHEAD)
    def _(c):
        stage_pick(c)

    acc_in[...] = jnp.zeros_like(acc_in)
    acc_out[...] = jnp.zeros_like(acc_out)
    macc[...] = jnp.zeros_like(macc)
    tacc[...] = jnp.zeros_like(tacc)
    loads[2].wait()
    loads[3].wait()

    stages = (
        (stage_f, 5),
        (stage_e, 4),
        (stage_d, 3),
        (stage_c, 2),
        (stage_b, 1),
        (stage_a, 0),
        (stage_g, 6),
        (combine, LAG),
    )

    def guarded(stage, c):
        @pl.when(jnp.logical_and(c >= 0, c < NCH))
        def _():
            stage(c)

    @pl.loop(0, NCH + 6)
    def _(s):
        for stage, lag in stages:
            guarded(stage, s - lag)
            if lag == 0:

                @pl.when(s == 0)
                def _():
                    peer_wait(rt2, pr.at[0])
                    peer_wait(gt2, pr.at[1])
                    find_slots(1, rt2, gt2)
                    peer_wait(tct.at[1], pr.at[2])

                for k in range(2):
                    guarded(stage_pick, AHEAD + 2 * s + k)

        done = s - 5

        @pl.when(
            jnp.logical_and(
                jnp.logical_and(done >= BATCH, done < NCH), lax.rem(done, BATCH) == 0
            )
        )
        def _():
            stage_h(done - BATCH)

        @pl.when(s == LAST_1 + LAG)
        def _():
            pout[0:W, :] = tacc[1, 0:W, :].astype(BF16)
            pout[W : 2 * W, :] = macc[1, 64:512, :].astype(BF16)
            to_peer(pout, pin, 3)

    stage_h(NCH - BATCH)
    wig_ref[...] = acc_in[0:W, :].astype(BF16)
    wog_ref[...] = acc_out[64:512, :].astype(BF16)
    peer_wait(pin, pr.at[3])

    @pl.loop(NCH + 6 - LAG, NCH)
    def _(c):
        combine(c)

    tgrad_ref[...] = (tacc[0, 0:W, :] + pin[0:W, :].astype(F32)).astype(BF16)
    mixed_ref[...] = (macc[0, 64:512, :] + pin[W : 2 * W, :].astype(F32)).astype(BF16)
    peer_wait(rt2, ps.at[0])
    peer_wait(gt2, ps.at[1])
    peer_wait(pin, ps.at[2])
    peer_wait(pin, ps.at[3])

    def sent(ref, c, k):
        pltpu.make_async_copy(ref, ref, ss.at[c, k]).wait()

    @pl.loop(0, NCH)
    def _(c):
        @pl.when(local(c))
        def _():
            sent(x0.at[c, 0], c, 0)
            sent(outb.at[c, 0], c, 15)

        @pl.when(jnp.logical_not(local(c)))
        def _():
            sent(x0.at[c], c, 0)
            sent(outb.at[c], c, 15)

        for k in range(1, 15):
            sent(sx.at[c], c, k)
        for k in (16, 23):
            sent(rf.at[c], c, k)
        for k in range(17, 23):
            sent(q1.at[c], c, k)


def shards(tokens, routing, gate_weights, cotangent, w_in, w_out):
    vmem = pl.BlockSpec(memory_space=pltpu.VMEM)
    hbm = pl.BlockSpec(memory_space=pl.ANY)
    dma = pltpu.SemaphoreType.DMA
    mixed, tgrad, wig, wog = pl.pallas_call(
        kernel,
        name="experts",
        out_shape=(
            pltpu.VMEM((W, TOK), BF16),
            pltpu.VMEM((W, TOK), BF16),
            pltpu.VMEM((W, 2 * H), BF16),
            pltpu.VMEM((W, H), BF16),
        ),
        in_specs=[hbm, hbm, vmem, vmem, hbm, hbm],
        out_specs=(vmem, vmem, vmem, vmem),
        scratch_shapes=[
            pltpu.VMEM((2, 2 * W, TOK), BF16),
            pltpu.VMEM((512, 2 * H), BF16),
            pltpu.VMEM((512, H), BF16),
            pltpu.VMEM((2, 16, 2, TOK), F32),
            pltpu.VMEM((2, 16, 2, TOK), F32),
            pltpu.VMEM((NCH, 2, CAP, 2 * W), BF16),
            pltpu.VMEM((NCH, 2, CAP, 2 * W), BF16),
            pltpu.VMEM((NCH, 4, 2, RY, BW), BF16),
            pltpu.VMEM((NCH, 2, RY, BW), BF16),
            pltpu.VMEM((NCH, 4, RY, BW), BF16),
            pltpu.VMEM((NCH, RY, BW), BF16),
            pltpu.VMEM((NCH, RY, BW), BF16),
            pltpu.VMEM((NCH, 4, 2, RY, BW), BF16),
            pltpu.VMEM((NCH, 2, 4, RX, BW), BF16),
            pltpu.VMEM((NCH, 4, RX, BW), BF16),
            pltpu.VMEM((NCH, RX, BW), BF16),
            pltpu.VMEM((NCH, 2, RX, BW), BF16),
            pltpu.VMEM((NCH, 2, 4, RX, BW), BF16),
            pltpu.VMEM((NCH, 2, CAP, 2 * W), BF16),
            pltpu.VMEM((NCH, 2, CAP, 2 * W), BF16),
            pltpu.VMEM((2 * W, BATCH * ROWS), BF16),
            pltpu.VMEM((512, 2 * H), F32),
            pltpu.VMEM((512, H), F32),
            pltpu.VMEM((2, 512, TOK), F32),
            pltpu.VMEM((2, 512, TOK), F32),
            pltpu.VMEM((8, TOK), jnp.int32),
            pltpu.VMEM((8, TOK), F32),
            pltpu.VMEM((2 * W, TOK), BF16),
            pltpu.VMEM((2 * W, TOK), BF16),
            dma((4,)),
            dma((4,)),
            dma((4,)),
            dma((NCH, 24)),
            dma((NCH, 24)),
        ],
        compiler_params=pltpu.CompilerParams(
            collective_id=0, has_side_effects=True, vmem_limit_bytes=57 << 20
        ),
    )(tokens.T, cotangent.T, routing.T, gate_weights.T, w_in[0], w_out[0].T)
    return mixed.T, tgrad.T, wig[None], wog.T[None]


def solution(mesh):
    placed = (
        P("expert", ("pipe", "dp")),
        P("expert", None),
        P("expert", None),
        P("expert", ("pipe", "dp")),
        P("expert", ("pipe", "dp"), None),
        P("expert", None, ("pipe", "dp")),
    )
    return jax.shard_map(
        shards,
        mesh=mesh,
        in_specs=placed,
        out_specs=(
            P("expert", ("pipe", "dp")),
            P("expert", ("pipe", "dp")),
            P("expert", ("pipe", "dp"), None),
            P("expert", None, ("pipe", "dp")),
        ),
        check_vma=False,
    )
```

```python
import jax
import jax.numpy as jnp
from jax import lax
from jax.experimental import pallas as pl
from jax.experimental.pallas import tpu as pltpu
from jax.sharding import PartitionSpec as P

H = 1024
CAP = 48
TOK = 128
W = 448
NZ = 8
NCH = 16
ROWS = 2 * CAP
RY = 64
RX = 32
BW = 384
AHEAD = 3
BATCH = 4
LAG = 10
ORDER = ((0, 0), (1, 0), (-2, 0), (0, 1), (1, 1), (-1, 1), (2, 1), (-2, 1))
ORDER += ((4, 1), (4, 0), (3, 1), (-3, 1), (3, 0), (-3, 0), (2, 0), (-1, 0))
LAST_1 = 11
LOCAL_1 = 3
MESH = pl.DeviceIdType.MESH
F32 = jnp.float32
BF16 = jnp.bfloat16


def nt_dot(a, b):
    return lax.dot_general(a, b, (((1,), (1,)), ((), ())), preferred_element_type=F32)


def tn_dot(a, b):
    return lax.dot_general(a, b, (((0,), (0,)), ((), ())), preferred_element_type=F32)


def dot(a, b):
    return jnp.dot(a, b, preferred_element_type=F32)


def kernel(
    tok_hbm,
    cot_hbm,
    rt_ref,
    gt_ref,
    win_hbm,
    wout_hbm,
    mixed_ref,
    tgrad_ref,
    wig_ref,
    wog_ref,
    tct,
    winp,
    woutp,
    code,
    gate,
    x0,
    xr,
    sb,
    r1,
    r2,
    sx,
    rx,
    g,
    sb2,
    rf,
    q1,
    q2,
    g2,
    outb,
    ret,
    xt,
    acc_in,
    acc_out,
    macc,
    tacc,
    rt2,
    gt2,
    pout,
    pin,
    w_sem,
    ps,
    pr,
    ss,
    rs,
):
    e, p, q = lax.axis_index("expert"), lax.axis_index("pipe"), lax.axis_index("dp")
    z, xhi, core = lax.div(e, 4), lax.rem(lax.div(e, 2), 2), lax.rem(e, 2)
    pu, pd, pf = lax.rem(p + 1, 4), lax.rem(p + 3, 4), lax.rem(p + 2, 4)
    up, dn, xp = (e, pu, q), (e, pd, q), (e, p, 1 - q)
    qo = 1 - q

    def send(src, dst, c, k, dev):
        pltpu.make_async_remote_copy(
            src_ref=src,
            dst_ref=dst,
            send_sem=ss.at[c, k],
            recv_sem=rs.at[c, k],
            device_id=dev,
            device_id_type=MESH,
        ).start()

    def wait(ref, c, k):
        pltpu.make_async_copy(ref, ref, rs.at[c, k]).wait()

    def place(c, sign):
        packed = jnp.int32(0)
        for i, (shift, half) in enumerate(ORDER):
            packed = jnp.where(c == i, 2 * (shift + NZ) + half, packed)
        shift, half = lax.div(packed, 2) - NZ, lax.rem(packed, 2)
        return 2 * lax.rem(z + sign * shift + NZ, NZ) + xhi, half

    barrier = pltpu.get_barrier_semaphore()
    peer = ((2 * z + 1 - xhi) * 2 + core, p, q)

    def greet(dev):
        pl.semaphore_signal(barrier, inc=1, device_id=dev, device_id_type=MESH)

    @pl.loop(0, 16)
    def _(d):
        other = (2 * lax.div(d, 2) + xhi) * 2 + lax.rem(d, 2)

        @pl.when(other != e)
        def _():
            greet((other, p, q))

    for dev in (up, dn, xp, peer):
        greet(dev)

    loads = [
        pltpu.make_async_copy(tok_hbm, tct.at[0, pl.ds(0, W)], w_sem.at[0]),
        pltpu.make_async_copy(cot_hbm, tct.at[0, pl.ds(W, W)], w_sem.at[1]),
        pltpu.make_async_copy(win_hbm, winp.at[pl.ds(0, W)], w_sem.at[2]),
        pltpu.make_async_copy(wout_hbm, woutp.at[pl.ds(64, W)], w_sem.at[3]),
    ]
    for load in loads:
        load.start()
    winp[pl.ds(W, 64), :] = jnp.zeros((64, 2 * H), BF16)
    woutp[pl.ds(0, 64), :] = jnp.zeros((64, H), BF16)

    ids = lax.broadcasted_iota(jnp.int32, (32, TOK), 0)
    before = jnp.where(
        lax.broadcasted_iota(jnp.int32, (TOK, TOK), 0)
        < lax.broadcasted_iota(jnp.int32, (TOK, TOK), 1),
        1.0,
        0.0,
    ).astype(BF16)

    def find_slots(half, rt, gt):
        hit = jnp.zeros((32, TOK), F32)
        weight = jnp.zeros((32, TOK), F32)
        for k in range(8):
            same = rt[k : k + 1, :] == ids
            hit = hit + jnp.where(same, 1.0, 0.0)
            weight = weight + jnp.where(same, gt[k : k + 1, :], 0.0)
        marked = jnp.where(hit > 0.5, dot(hit.astype(BF16), before), -1.0)
        for i in range(16):
            code[half, i, :, :] = marked[2 * i : 2 * i + 2, :]
            gate[half, i, :, :] = weight[2 * i : 2 * i + 2, :]

    find_slots(0, rt_ref, gt_ref)

    row_ids = lax.broadcasted_iota(jnp.int32, (CAP, TOK), 0).astype(F32)
    lanes = lax.broadcasted_iota(jnp.int32, (ROWS, 2 * W), 1)

    def picks(at, half):
        cq, gq = code[half, at], gate[half, at]
        chosen = [cq[j : j + 1, :] == row_ids for j in range(2)]
        pick = [jnp.where(m, 1.0, 0.0) for m in chosen]
        gates = [jnp.where(m, gq[j : j + 1, :], 0.0) for j, m in enumerate(chosen)]
        return jnp.concatenate(pick, axis=0), jnp.concatenate(gates, axis=0)

    def local(c):
        return jnp.logical_or(c == 0, c == LOCAL_1)

    def deliver(src, dst, c, k, at):
        for j in range(2):
            own = jnp.logical_and(local(c), core == j)

            @pl.when(own)
            def _():
                pltpu.make_async_copy(src.at[c, j], dst.at[c, core], rs.at[c, k]).start()

            @pl.when(jnp.logical_not(own))
            def _():
                send(src.at[c, j], dst.at[c, core], c, k, (at * 2 + j, p, q))

    def stage_pick(c):
        at, half = place(c, 1)
        pick, gates = picks(at, half)
        row_gate = jnp.sum(gates, axis=1, keepdims=True)
        rows = nt_dot(pick.astype(BF16), tct[half])
        rows = jnp.where(lanes >= W, rows * row_gate, rows).astype(BF16)
        x0[c] = rows.reshape(2, CAP, 2 * W)
        deliver(x0, xr, c, 0, at)

    def stage_a(c):
        wait(xr.at[c], c, 0)
        rows = xr[c].reshape(ROWS, 2 * W)
        x, dy = rows[:, 0:512], rows[:, 384:896]
        for k, pp in enumerate((pf, pu, pd, p)):
            at = pl.multiple_of(pp * 256, 256)
            gp = dot(x, winp[:, pl.ds(at, 256)]).astype(BF16)
            un = dot(x, winp[:, pl.ds(at + H, 256)]).astype(BF16)
            bk = dot(dy, woutp[:, pl.ds(at, 256)]).astype(BF16)
            for h in range(2):
                s = slice(h * 128, h * 128 + 128)
                for i, v in enumerate((gp, un, bk)):
                    t = slice(i * 128, i * 128 + 128)
                    sb[c, pp, h, :, t] = v[0:RY, s]
                    sb2[c, h, pp, :, t] = v[RY:ROWS, s]
            if k == 0:
                send(sb.at[c, pf, 0], r1.at[c, 0], c, 1, up)
                send(sb.at[c, pf, 1], r1.at[c, 1], c, 2, dn)
            if k == 1:
                send(sb.at[c, pu, 1], r2.at[c, 0], c, 3, up)
            if k == 2:
                send(sb.at[c, pd, 0], r2.at[c, 1], c, 4, dn)
        send(sb2.at[c, qo], rf.at[c], c, 16, xp)

    def by_parity(c, run):
        @pl.when(lax.rem(c, 2) == 0)
        def _():
            run(up, pu, dn, pd)

        @pl.when(lax.rem(c, 2) == 1)
        def _():
            run(dn, pd, up, pu)

    def stage_b(c):
        wait(r1.at[c, 0], c, 1)
        sb[c, pu, 0] = (sb[c, pu, 0].astype(F32) + r1[c, 0].astype(F32)).astype(BF16)
        send(sb.at[c, pu, 0], r2.at[c, 2], c, 5, up)
        wait(r1.at[c, 1], c, 2)
        sb[c, pd, 1] = (sb[c, pd, 1].astype(F32) + r1[c, 1].astype(F32)).astype(BF16)
        send(sb.at[c, pd, 1], r2.at[c, 3], c, 6, dn)
        wait(rf.at[c], c, 16)
        sb2[c, q] = (sb2[c, q].astype(F32) + rf[c].astype(F32)).astype(BF16)

        def run(a, pa, b, pb):
            send(sb2.at[c, q, pf], q1.at[c], c, 17, a)
            send(sb2.at[c, q, pb], q2.at[c, 1], c, 18, b)

        by_parity(c, run)

    def y_sum(c, h):
        return (
            sb[c, p, h].astype(F32)
            + r2[c, 1 - h].astype(F32)
            + r2[c, 2 + h].astype(F32)
        )

    def stage_c(c):
        for k in range(4):
            wait(r2.at[c, k], c, 3 + k)
        sx[c] = y_sum(c, qo).astype(BF16)
        send(sx.at[c], rx.at[c], c, 7, xp)
        wait(q1.at[c], c, 17)

        def run(a, pa, b, pb):
            sb2[c, q, pa] = (sb2[c, q, pa].astype(F32) + q1[c].astype(F32)).astype(BF16)
            send(sb2.at[c, q, pa], q2.at[c, 0], c, 19, a)

        by_parity(c, run)

    def activate(total):
        gp, un, bk = total[:, 0:128], total[:, 128:256], total[:, 256:384]
        s = 1.0 / (1.0 + jnp.exp(-gp))
        act = gp * s
        return jnp.concatenate(
            [act * un, bk * un * (s * (1.0 + gp * (1.0 - s))), bk * act], axis=1
        ).astype(BF16)

    def stage_d(c):
        wait(rx.at[c], c, 7)
        g[c, p, q] = activate(y_sum(c, q) + rx[c].astype(F32))
        mine = g.at[c, p, q]
        send(mine, mine, c, 8, xp)
        send(mine, mine, c, 9, up)
        send(mine, mine, c, 10, dn)
        wait(q2.at[c, 1], c, 18)
        wait(q2.at[c, 0], c, 19)
        g2[c, q, p] = activate(
            sb2[c, q, p].astype(F32) + q2[c, 0].astype(F32) + q2[c, 1].astype(F32)
        )
        mine2 = g2.at[c, q, p]
        send(mine2, mine2, c, 20, up)
        send(mine2, mine2, c, 21, dn)

    def stage_e(c):
        other = g.at[c, p, qo]
        wait(other, c, 8)
        send(other, other, c, 11, up)
        send(other, other, c, 12, dn)
        wait(g2.at[c, q, pd], c, 20)
        wait(g2.at[c, q, pu], c, 21)

        def run(a, pa, b, pb):
            send(g2.at[c, q, pb], g2.at[c, q, pb], c, 22, a)

        by_parity(c, run)

    def stage_f(c):
        wait(g.at[c, pd, q], c, 9)
        wait(g.at[c, pu, q], c, 10)
        wait(g.at[c, pd, qo], c, 11)
        wait(g.at[c, pu, qo], c, 12)
        send(g.at[c, pd, 0], g.at[c, pd, 0], c, 13, up)
        send(g.at[c, pu, 1], g.at[c, pu, 1], c, 14, dn)
        wait(g2.at[c, q, pf], c, 22)
        send(g2.at[c, q], g2.at[c, q], c, 23, xp)

    def stage_g(c):
        wait(g.at[c, pf, 0], c, 13)
        wait(g.at[c, pf, 1], c, 14)
        wait(g2.at[c, qo], c, 23)

        def part(k):
            s = slice(k * 128, k * 128 + 128)
            y = [g[c, i // 2, i % 2, :, s] for i in range(8)]
            x = [g2[c, i % 2, i // 2, :, s] for i in range(8)]
            return jnp.concatenate(
                [jnp.concatenate(y, axis=1), jnp.concatenate(x, axis=1)], axis=0
            )

        back = nt_dot(part(1), winp[:, 0:H]) + nt_dot(part(2), winp[:, H : 2 * H])
        out = nt_dot(part(0), woutp[...])
        for j in range(2):
            s = slice(j * CAP, j * CAP + CAP)
            outb[c, j, :, 0:384] = back[s, 0:384].astype(BF16)
            outb[c, j, :, 384:512] = (back[s, 384:512] + out[s, 0:128]).astype(BF16)
            outb[c, j, :, 512:896] = out[s, 128:512].astype(BF16)
        deliver(outb, ret, c, 15, place(c, -1)[0])

    def stage_h(first):
        rows = xr[pl.ds(first, BATCH)].reshape(BATCH * ROWS, 2 * W)
        xt[...] = rows.T

        @pl.loop(0, 4)
        def _(pp):
            def pair(k):
                s = slice(k * 128, k * 128 + 128)
                parts = []
                for b in range(BATCH):
                    c = first + b
                    y = [g[c, pp, h, :, s] for h in range(2)]
                    x = [g2[c, h, pp, :, s] for h in range(2)]
                    parts += [jnp.concatenate(y, axis=1), jnp.concatenate(x, axis=1)]
                return jnp.concatenate(parts, axis=0)

            at = pl.multiple_of(pp * 256, 256)
            acc_in[:, pl.ds(at, 256)] += dot(xt[0:512, :], pair(1))
            acc_in[:, pl.ds(at + H, 256)] += dot(xt[0:512, :], pair(2))
            acc_out[:, pl.ds(at, 256)] += dot(xt[384:896, :], pair(0))

    def combine(c):
        wait(ret.at[c], c, 15)
        at, half = place(c, 1)
        pick, gates = picks(at, half)
        rows = ret[c].reshape(ROWS, 2 * W)
        high = gates.astype(BF16)
        low = (gates - high.astype(F32)).astype(BF16)
        tacc[half] += tn_dot(rows[:, 0:512], pick.astype(BF16))
        macc[half] += tn_dot(rows[:, 384:896], high) + tn_dot(rows[:, 384:896], low)

    loads[0].wait()
    loads[1].wait()
    pl.semaphore_wait(barrier, 19)

    def to_peer(src, dst, k):
        pltpu.make_async_remote_copy(
            src_ref=src,
            dst_ref=dst,
            send_sem=ps.at[k],
            recv_sem=pr.at[k],
            device_id=peer,
            device_id_type=MESH,
        ).start()

    def peer_wait(ref, sem):
        pltpu.make_async_copy(ref, ref, sem).wait()

    to_peer(rt_ref, rt2, 0)
    to_peer(gt_ref, gt2, 1)
    to_peer(tct.at[0], tct.at[1], 2)

    @pl.loop(0, AHEAD)
    def _(c):
        stage_pick(c)

    acc_in[...] = jnp.zeros_like(acc_in)
    acc_out[...] = jnp.zeros_like(acc_out)
    macc[...] = jnp.zeros_like(macc)
    tacc[...] = jnp.zeros_like(tacc)
    loads[2].wait()
    loads[3].wait()

    stages = (
        (stage_g, 6),
        (stage_f, 5),
        (stage_e, 4),
        (stage_d, 3),
        (stage_c, 2),
        (stage_b, 1),
        (stage_a, 0),
        (combine, LAG),
    )

    def guarded(stage, c):
        @pl.when(jnp.logical_and(c >= 0, c < NCH))
        def _():
            stage(c)

    @pl.loop(0, NCH + 6)
    def _(s):
        for stage, lag in stages:
            guarded(stage, s - lag)
            if lag == 0:

                @pl.when(s == 0)
                def _():
                    peer_wait(rt2, pr.at[0])
                    peer_wait(gt2, pr.at[1])
                    find_slots(1, rt2, gt2)
                    peer_wait(tct.at[1], pr.at[2])

                for k in range(2):
                    guarded(stage_pick, AHEAD + 2 * s + k)

        done = s - 5

        @pl.when(
            jnp.logical_and(
                jnp.logical_and(done >= BATCH, done < NCH - BATCH), lax.rem(done, BATCH) == 0
            )
        )
        def _():
            stage_h(done - BATCH)

        @pl.when(s == LAST_1 + LAG)
        def _():
            pout[0:W, :] = tacc[1, 0:W, :].astype(BF16)
            pout[W : 2 * W, :] = macc[1, 64:512, :].astype(BF16)
            to_peer(pout, pin, 3)

    stage_h(NCH - 2 * BATCH)
    stage_h(NCH - BATCH)
    wig_ref[...] = acc_in[0:W, :].astype(BF16)
    wog_ref[...] = acc_out[64:512, :].astype(BF16)
    peer_wait(pin, pr.at[3])

    @pl.loop(NCH + 6 - LAG, NCH)
    def _(c):
        combine(c)

    tgrad_ref[...] = (tacc[0, 0:W, :] + pin[0:W, :].astype(F32)).astype(BF16)
    mixed_ref[...] = (macc[0, 64:512, :] + pin[W : 2 * W, :].astype(F32)).astype(BF16)
    peer_wait(rt2, ps.at[0])
    peer_wait(gt2, ps.at[1])
    peer_wait(pin, ps.at[2])
    peer_wait(pin, ps.at[3])

    def sent(ref, c, k):
        pltpu.make_async_copy(ref, ref, ss.at[c, k]).wait()

    @pl.loop(0, NCH)
    def _(c):
        @pl.when(local(c))
        def _():
            sent(x0.at[c, 0], c, 0)
            sent(outb.at[c, 0], c, 15)

        @pl.when(jnp.logical_not(local(c)))
        def _():
            sent(x0.at[c], c, 0)
            sent(outb.at[c], c, 15)

        for k in range(1, 15):
            sent(sx.at[c], c, k)
        for k in (16, 23):
            sent(rf.at[c], c, k)
        for k in range(17, 23):
            sent(q1.at[c], c, k)


def shards(tokens, routing, gate_weights, cotangent, w_in, w_out):
    vmem = pl.BlockSpec(memory_space=pltpu.VMEM)
    hbm = pl.BlockSpec(memory_space=pl.ANY)
    dma = pltpu.SemaphoreType.DMA
    mixed, tgrad, wig, wog = pl.pallas_call(
        kernel,
        name="experts",
        out_shape=(
            pltpu.VMEM((W, TOK), BF16),
            pltpu.VMEM((W, TOK), BF16),
            pltpu.VMEM((W, 2 * H), BF16),
            pltpu.VMEM((W, H), BF16),
        ),
        in_specs=[hbm, hbm, vmem, vmem, hbm, hbm],
        out_specs=(vmem, vmem, vmem, vmem),
        scratch_shapes=[
            pltpu.VMEM((2, 2 * W, TOK), BF16),
            pltpu.VMEM((512, 2 * H), BF16),
            pltpu.VMEM((512, H), BF16),
            pltpu.VMEM((2, 16, 2, TOK), F32),
            pltpu.VMEM((2, 16, 2, TOK), F32),
            pltpu.VMEM((NCH, 2, CAP, 2 * W), BF16),
            pltpu.VMEM((NCH, 2, CAP, 2 * W), BF16),
            pltpu.VMEM((NCH, 4, 2, RY, BW), BF16),
            pltpu.VMEM((NCH, 2, RY, BW), BF16),
            pltpu.VMEM((NCH, 4, RY, BW), BF16),
            pltpu.VMEM((NCH, RY, BW), BF16),
            pltpu.VMEM((NCH, RY, BW), BF16),
            pltpu.VMEM((NCH, 4, 2, RY, BW), BF16),
            pltpu.VMEM((NCH, 2, 4, RX, BW), BF16),
            pltpu.VMEM((NCH, 4, RX, BW), BF16),
            pltpu.VMEM((NCH, RX, BW), BF16),
            pltpu.VMEM((NCH, 2, RX, BW), BF16),
            pltpu.VMEM((NCH, 2, 4, RX, BW), BF16),
            pltpu.VMEM((NCH, 2, CAP, 2 * W), BF16),
            pltpu.VMEM((NCH, 2, CAP, 2 * W), BF16),
            pltpu.VMEM((2 * W, BATCH * ROWS), BF16),
            pltpu.VMEM((512, 2 * H), F32),
            pltpu.VMEM((512, H), F32),
            pltpu.VMEM((2, 512, TOK), F32),
            pltpu.VMEM((2, 512, TOK), F32),
            pltpu.VMEM((8, TOK), jnp.int32),
            pltpu.VMEM((8, TOK), F32),
            pltpu.VMEM((2 * W, TOK), BF16),
            pltpu.VMEM((2 * W, TOK), BF16),
            dma((4,)),
            dma((4,)),
            dma((4,)),
            dma((NCH, 24)),
            dma((NCH, 24)),
        ],
        compiler_params=pltpu.CompilerParams(
            collective_id=0, has_side_effects=True, vmem_limit_bytes=57 << 20
        ),
    )(tokens.T, cotangent.T, routing.T, gate_weights.T, w_in[0], w_out[0].T)
    return mixed.T, tgrad.T, wig[None], wog.T[None]


def solution(mesh):
    placed = (
        P("expert", ("pipe", "dp")),
        P("expert", None),
        P("expert", None),
        P("expert", ("pipe", "dp")),
        P("expert", ("pipe", "dp"), None),
        P("expert", None, ("pipe", "dp")),
    )
    return jax.shard_map(
        shards,
        mesh=mesh,
        in_specs=placed,
        out_specs=(
            P("expert", ("pipe", "dp")),
            P("expert", ("pipe", "dp")),
            P("expert", ("pipe", "dp"), None),
            P("expert", None, ("pipe", "dp")),
        ),
        check_vma=False,
    )
```

```python
import jax
import jax.numpy as jnp
from jax import lax
from jax.experimental import pallas as pl
from jax.experimental.pallas import tpu as pltpu
from jax.sharding import PartitionSpec as P

H = 1024
CAP = 48
TOK = 128
W = 448
NZ = 8
NCH = 16
ROWS = 2 * CAP
RY = 64
RX = 32
BW = 384
AHEAD = 3
BATCH = 4
LAG = 10
ORDER = ((0, 0), (1, 0), (-2, 0), (0, 1), (1, 1), (-1, 1), (2, 1), (-2, 1))
ORDER += ((4, 1), (4, 0), (3, 1), (-3, 1), (3, 0), (-3, 0), (2, 0), (-1, 0))
LAST_1 = 11
LOCAL_1 = 3
MESH = pl.DeviceIdType.MESH
F32 = jnp.float32
BF16 = jnp.bfloat16


def nt_dot(a, b):
    return lax.dot_general(a, b, (((1,), (1,)), ((), ())), preferred_element_type=F32)


def tn_dot(a, b):
    return lax.dot_general(a, b, (((0,), (0,)), ((), ())), preferred_element_type=F32)


def dot(a, b):
    return jnp.dot(a, b, preferred_element_type=F32)


def kernel(
    tok_hbm,
    cot_hbm,
    rt_ref,
    gt_ref,
    win_hbm,
    wout_hbm,
    mixed_ref,
    tgrad_ref,
    wig_ref,
    wog_ref,
    tct,
    winp,
    woutp,
    code,
    gate,
    x0,
    xr,
    sb,
    r1,
    r2,
    sx,
    rx,
    g,
    sb2,
    rf,
    q1,
    q2,
    g2,
    outb,
    ret,
    xt,
    acc_in,
    acc_out,
    macc,
    tacc,
    rt2,
    gt2,
    pout,
    pin,
    w_sem,
    ps,
    pr,
    ss,
    rs,
):
    e, p, q = lax.axis_index("expert"), lax.axis_index("pipe"), lax.axis_index("dp")
    z, xhi, core = lax.div(e, 4), lax.rem(lax.div(e, 2), 2), lax.rem(e, 2)
    pu, pd, pf = lax.rem(p + 1, 4), lax.rem(p + 3, 4), lax.rem(p + 2, 4)
    up, dn, xp = (e, pu, q), (e, pd, q), (e, p, 1 - q)
    qo = 1 - q

    def send(src, dst, c, k, dev):
        pltpu.make_async_remote_copy(
            src_ref=src,
            dst_ref=dst,
            send_sem=ss.at[c, k],
            recv_sem=rs.at[c, k],
            device_id=dev,
            device_id_type=MESH,
        ).start()

    def wait(ref, c, k):
        pltpu.make_async_copy(ref, ref, rs.at[c, k]).wait()

    def place(c, sign):
        packed = jnp.int32(0)
        for i, (shift, half) in enumerate(ORDER):
            packed = jnp.where(c == i, 2 * (shift + NZ) + half, packed)
        shift, half = lax.div(packed, 2) - NZ, lax.rem(packed, 2)
        return 2 * lax.rem(z + sign * shift + NZ, NZ) + xhi, half

    barrier = pltpu.get_barrier_semaphore()
    peer = ((2 * z + 1 - xhi) * 2 + core, p, q)

    def greet(dev):
        pl.semaphore_signal(barrier, inc=1, device_id=dev, device_id_type=MESH)

    @pl.loop(0, 16)
    def _(d):
        other = (2 * lax.div(d, 2) + xhi) * 2 + lax.rem(d, 2)

        @pl.when(other != e)
        def _():
            greet((other, p, q))

    for dev in (up, dn, xp, peer):
        greet(dev)

    loads = [
        pltpu.make_async_copy(tok_hbm, tct.at[0, pl.ds(0, W)], w_sem.at[0]),
        pltpu.make_async_copy(cot_hbm, tct.at[0, pl.ds(W, W)], w_sem.at[1]),
        pltpu.make_async_copy(win_hbm, winp.at[pl.ds(0, W)], w_sem.at[2]),
        pltpu.make_async_copy(wout_hbm, woutp.at[pl.ds(64, W)], w_sem.at[3]),
    ]
    for load in loads:
        load.start()
    winp[pl.ds(W, 64), :] = jnp.zeros((64, 2 * H), BF16)
    woutp[pl.ds(0, 64), :] = jnp.zeros((64, H), BF16)

    ids = lax.broadcasted_iota(jnp.int32, (32, TOK), 0)
    before = jnp.where(
        lax.broadcasted_iota(jnp.int32, (TOK, TOK), 0)
        < lax.broadcasted_iota(jnp.int32, (TOK, TOK), 1),
        1.0,
        0.0,
    ).astype(BF16)

    def find_slots(half, rt, gt):
        hit = jnp.zeros((32, TOK), F32)
        weight = jnp.zeros((32, TOK), F32)
        for k in range(8):
            same = rt[k : k + 1, :] == ids
            hit = hit + jnp.where(same, 1.0, 0.0)
            weight = weight + jnp.where(same, gt[k : k + 1, :], 0.0)
        marked = jnp.where(hit > 0.5, dot(hit.astype(BF16), before), -1.0)
        for i in range(16):
            code[half, i, :, :] = marked[2 * i : 2 * i + 2, :]
            gate[half, i, :, :] = weight[2 * i : 2 * i + 2, :]

    find_slots(0, rt_ref, gt_ref)

    row_ids = lax.broadcasted_iota(jnp.int32, (CAP, TOK), 0).astype(F32)
    lanes = lax.broadcasted_iota(jnp.int32, (ROWS, 2 * W), 1)

    def picks(at, half):
        cq, gq = code[half, at], gate[half, at]
        chosen = [cq[j : j + 1, :] == row_ids for j in range(2)]
        pick = [jnp.where(m, 1.0, 0.0) for m in chosen]
        gates = [jnp.where(m, gq[j : j + 1, :], 0.0) for j, m in enumerate(chosen)]
        return jnp.concatenate(pick, axis=0), jnp.concatenate(gates, axis=0)

    def local(c):
        return jnp.logical_or(c == 0, c == LOCAL_1)

    def deliver(src, dst, c, k, at):
        for j in range(2):
            own = jnp.logical_and(local(c), core == j)

            @pl.when(own)
            def _():
                pltpu.make_async_copy(src.at[c, j], dst.at[c, core], rs.at[c, k]).start()

            @pl.when(jnp.logical_not(own))
            def _():
                send(src.at[c, j], dst.at[c, core], c, k, (at * 2 + j, p, q))

    def stage_pick(c):
        at, half = place(c, 1)
        pick, gates = picks(at, half)
        row_gate = jnp.sum(gates, axis=1, keepdims=True)
        rows = nt_dot(pick.astype(BF16), tct[half])
        rows = jnp.where(lanes >= W, rows * row_gate, rows).astype(BF16)
        x0[c] = rows.reshape(2, CAP, 2 * W)
        deliver(x0, xr, c, 0, at)

    def stage_a(c):
        wait(xr.at[c], c, 0)
        rows = xr[c].reshape(ROWS, 2 * W)
        x, dy = rows[:, 0:512], rows[:, 384:896]
        for k, pp in enumerate((pf, pu, pd, p)):
            at = pl.multiple_of(pp * 256, 256)
            gp = dot(x, winp[:, pl.ds(at, 256)]).astype(BF16)
            un = dot(x, winp[:, pl.ds(at + H, 256)]).astype(BF16)
            bk = dot(dy, woutp[:, pl.ds(at, 256)]).astype(BF16)
            for h in range(2):
                s = slice(h * 128, h * 128 + 128)
                for i, v in enumerate((gp, un, bk)):
                    t = slice(i * 128, i * 128 + 128)
                    sb[c, pp, h, :, t] = v[0:RY, s]
                    sb2[c, h, pp, :, t] = v[RY:ROWS, s]
            if k == 0:
                send(sb.at[c, pf, 0], r1.at[c, 0], c, 1, up)
                send(sb.at[c, pf, 1], r1.at[c, 1], c, 2, dn)
            if k == 1:
                send(sb.at[c, pu, 1], r2.at[c, 0], c, 3, up)
            if k == 2:
                send(sb.at[c, pd, 0], r2.at[c, 1], c, 4, dn)
        send(sb2.at[c, qo], rf.at[c], c, 16, xp)

    def by_parity(c, run):
        @pl.when(lax.rem(c, 2) == 0)
        def _():
            run(up, pu, dn, pd)

        @pl.when(lax.rem(c, 2) == 1)
        def _():
            run(dn, pd, up, pu)

    def stage_b(c):
        wait(r1.at[c, 0], c, 1)
        sb[c, pu, 0] = (sb[c, pu, 0].astype(F32) + r1[c, 0].astype(F32)).astype(BF16)
        send(sb.at[c, pu, 0], r2.at[c, 2], c, 5, up)
        wait(r1.at[c, 1], c, 2)
        sb[c, pd, 1] = (sb[c, pd, 1].astype(F32) + r1[c, 1].astype(F32)).astype(BF16)
        send(sb.at[c, pd, 1], r2.at[c, 3], c, 6, dn)
        wait(rf.at[c], c, 16)
        sb2[c, q] = (sb2[c, q].astype(F32) + rf[c].astype(F32)).astype(BF16)

        def run(a, pa, b, pb):
            send(sb2.at[c, q, pf], q1.at[c], c, 17, a)
            send(sb2.at[c, q, pb], q2.at[c, 1], c, 18, b)

        by_parity(c, run)

    def y_sum(c, h):
        return (
            sb[c, p, h].astype(F32)
            + r2[c, 1 - h].astype(F32)
            + r2[c, 2 + h].astype(F32)
        )

    def stage_c(c):
        for k in range(4):
            wait(r2.at[c, k], c, 3 + k)
        sx[c] = y_sum(c, qo).astype(BF16)
        send(sx.at[c], rx.at[c], c, 7, xp)
        wait(q1.at[c], c, 17)

        def run(a, pa, b, pb):
            sb2[c, q, pa] = (sb2[c, q, pa].astype(F32) + q1[c].astype(F32)).astype(BF16)
            send(sb2.at[c, q, pa], q2.at[c, 0], c, 19, a)

        by_parity(c, run)

    def activate(total):
        gp, un, bk = total[:, 0:128], total[:, 128:256], total[:, 256:384]
        s = 1.0 / (1.0 + jnp.exp(-gp))
        act = gp * s
        return jnp.concatenate(
            [act * un, bk * un * (s * (1.0 + gp * (1.0 - s))), bk * act], axis=1
        ).astype(BF16)

    def stage_d(c):
        wait(rx.at[c], c, 7)
        g[c, p, q] = activate(y_sum(c, q) + rx[c].astype(F32))
        mine = g.at[c, p, q]
        send(mine, mine, c, 8, xp)
        send(mine, mine, c, 9, up)
        send(mine, mine, c, 10, dn)
        wait(q2.at[c, 1], c, 18)
        wait(q2.at[c, 0], c, 19)
        g2[c, q, p] = activate(
            sb2[c, q, p].astype(F32) + q2[c, 0].astype(F32) + q2[c, 1].astype(F32)
        )
        mine2 = g2.at[c, q, p]
        send(mine2, mine2, c, 20, up)
        send(mine2, mine2, c, 21, dn)

    def stage_e(c):
        other = g.at[c, p, qo]
        wait(other, c, 8)
        send(other, other, c, 11, up)
        send(other, other, c, 12, dn)
        wait(g2.at[c, q, pd], c, 20)
        wait(g2.at[c, q, pu], c, 21)

        def run(a, pa, b, pb):
            send(g2.at[c, q, pb], g2.at[c, q, pb], c, 22, a)

        by_parity(c, run)

    def stage_f(c):
        wait(g.at[c, pd, q], c, 9)
        wait(g.at[c, pu, q], c, 10)
        wait(g.at[c, pd, qo], c, 11)
        wait(g.at[c, pu, qo], c, 12)
        send(g.at[c, pd, 0], g.at[c, pd, 0], c, 13, up)
        send(g.at[c, pu, 1], g.at[c, pu, 1], c, 14, dn)
        wait(g2.at[c, q, pf], c, 22)
        send(g2.at[c, q], g2.at[c, q], c, 23, xp)

    def stage_g(c):
        wait(g.at[c, pf, 0], c, 13)
        wait(g.at[c, pf, 1], c, 14)
        wait(g2.at[c, qo], c, 23)

        def part(k):
            s = slice(k * 128, k * 128 + 128)
            y = [g[c, i // 2, i % 2, :, s] for i in range(8)]
            x = [g2[c, i % 2, i // 2, :, s] for i in range(8)]
            return jnp.concatenate(
                [jnp.concatenate(y, axis=1), jnp.concatenate(x, axis=1)], axis=0
            )

        back = nt_dot(part(1), winp[:, 0:H]) + nt_dot(part(2), winp[:, H : 2 * H])
        out = nt_dot(part(0), woutp[...])
        for j in range(2):
            s = slice(j * CAP, j * CAP + CAP)
            outb[c, j, :, 0:384] = back[s, 0:384].astype(BF16)
            outb[c, j, :, 384:512] = (back[s, 384:512] + out[s, 0:128]).astype(BF16)
            outb[c, j, :, 512:896] = out[s, 128:512].astype(BF16)
        deliver(outb, ret, c, 15, place(c, -1)[0])

    def stage_h(first, count=BATCH, last=False):
        depth = count * ROWS
        xt[:, 0:depth] = xr[pl.ds(first, count)].reshape(depth, 2 * W).T

        @pl.loop(0, 4)
        def _(pp):
            def pair(k):
                s = slice(k * 128, k * 128 + 128)
                parts = []
                for b in range(count):
                    c = first + b
                    y = [g[c, pp, h, :, s] for h in range(2)]
                    x = [g2[c, h, pp, :, s] for h in range(2)]
                    parts += [jnp.concatenate(y, axis=1), jnp.concatenate(x, axis=1)]
                return jnp.concatenate(parts, axis=0)

            at = pl.multiple_of(pp * 256, 256)
            left, right = xt[0:512, 0:depth], xt[384:896, 0:depth]
            in_gate = acc_in[:, pl.ds(at, 256)] + dot(left, pair(1))
            in_up = acc_in[:, pl.ds(at + H, 256)] + dot(left, pair(2))
            out = acc_out[:, pl.ds(at, 256)] + dot(right, pair(0))
            if last:
                wig_ref[:, pl.ds(at, 256)] = in_gate[0:W, :].astype(BF16)
                wig_ref[:, pl.ds(at + H, 256)] = in_up[0:W, :].astype(BF16)
                wog_ref[:, pl.ds(at, 256)] = out[64:512, :].astype(BF16)
            else:
                acc_in[:, pl.ds(at, 256)] = in_gate
                acc_in[:, pl.ds(at + H, 256)] = in_up
                acc_out[:, pl.ds(at, 256)] = out

    def combine(c):
        wait(ret.at[c], c, 15)
        at, half = place(c, 1)
        pick, gates = picks(at, half)
        rows = ret[c].reshape(ROWS, 2 * W)
        high = gates.astype(BF16)
        low = (gates - high.astype(F32)).astype(BF16)
        tacc[half] += tn_dot(rows[:, 0:512], pick.astype(BF16))
        macc[half] += tn_dot(rows[:, 384:896], high) + tn_dot(rows[:, 384:896], low)

    loads[0].wait()
    loads[1].wait()
    pl.semaphore_wait(barrier, 19)

    def to_peer(src, dst, k):
        pltpu.make_async_remote_copy(
            src_ref=src,
            dst_ref=dst,
            send_sem=ps.at[k],
            recv_sem=pr.at[k],
            device_id=peer,
            device_id_type=MESH,
        ).start()

    def peer_wait(ref, sem):
        pltpu.make_async_copy(ref, ref, sem).wait()

    to_peer(rt_ref, rt2, 0)
    to_peer(gt_ref, gt2, 1)
    to_peer(tct.at[0], tct.at[1], 2)

    @pl.loop(0, AHEAD)
    def _(c):
        stage_pick(c)

    acc_in[...] = jnp.zeros_like(acc_in)
    acc_out[...] = jnp.zeros_like(acc_out)
    macc[...] = jnp.zeros_like(macc)
    tacc[...] = jnp.zeros_like(tacc)
    loads[2].wait()
    loads[3].wait()

    stages = (
        (stage_g, 6),
        (stage_f, 5),
        (stage_e, 4),
        (stage_d, 3),
        (stage_c, 2),
        (stage_b, 1),
        (stage_a, 0),
        (combine, LAG),
    )

    def guarded(stage, c):
        @pl.when(jnp.logical_and(c >= 0, c < NCH))
        def _():
            stage(c)

    @pl.loop(0, NCH + 6)
    def _(s):
        for stage, lag in stages:
            guarded(stage, s - lag)
            if lag == 0:

                @pl.when(s == 0)
                def _():
                    peer_wait(rt2, pr.at[0])
                    peer_wait(gt2, pr.at[1])
                    find_slots(1, rt2, gt2)
                    peer_wait(tct.at[1], pr.at[2])

                for k in range(2):
                    guarded(stage_pick, AHEAD + 2 * s + k)

        done = s - 5

        @pl.when(
            jnp.logical_and(
                jnp.logical_and(done >= BATCH, done < NCH - BATCH), lax.rem(done, BATCH) == 0
            )
        )
        def _():
            stage_h(done - BATCH)

        @pl.when(s == LAST_1 + LAG)
        def _():
            pout[0:W, :] = tacc[1, 0:W, :].astype(BF16)
            pout[W : 2 * W, :] = macc[1, 64:512, :].astype(BF16)
            to_peer(pout, pin, 3)

    stage_h(NCH - 2 * BATCH, 2 * BATCH, True)
    peer_wait(pin, pr.at[3])

    @pl.loop(NCH + 6 - LAG, NCH)
    def _(c):
        combine(c)

    tgrad_ref[...] = (tacc[0, 0:W, :] + pin[0:W, :].astype(F32)).astype(BF16)
    mixed_ref[...] = (macc[0, 64:512, :] + pin[W : 2 * W, :].astype(F32)).astype(BF16)
    peer_wait(rt2, ps.at[0])
    peer_wait(gt2, ps.at[1])
    peer_wait(pin, ps.at[2])
    peer_wait(pin, ps.at[3])

    def sent(ref, c, k):
        pltpu.make_async_copy(ref, ref, ss.at[c, k]).wait()

    @pl.loop(0, NCH)
    def _(c):
        @pl.when(local(c))
        def _():
            sent(x0.at[c, 0], c, 0)
            sent(outb.at[c, 0], c, 15)

        @pl.when(jnp.logical_not(local(c)))
        def _():
            sent(x0.at[c], c, 0)
            sent(outb.at[c], c, 15)

        for k in range(1, 15):
            sent(sx.at[c], c, k)
        for k in (16, 23):
            sent(rf.at[c], c, k)
        for k in range(17, 23):
            sent(q1.at[c], c, k)


def shards(tokens, routing, gate_weights, cotangent, w_in, w_out):
    vmem = pl.BlockSpec(memory_space=pltpu.VMEM)
    hbm = pl.BlockSpec(memory_space=pl.ANY)
    dma = pltpu.SemaphoreType.DMA
    mixed, tgrad, wig, wog = pl.pallas_call(
        kernel,
        name="experts",
        out_shape=(
            pltpu.VMEM((W, TOK), BF16),
            pltpu.VMEM((W, TOK), BF16),
            pltpu.VMEM((W, 2 * H), BF16),
            pltpu.VMEM((W, H), BF16),
        ),
        in_specs=[hbm, hbm, vmem, vmem, hbm, hbm],
        out_specs=(vmem, vmem, vmem, vmem),
        scratch_shapes=[
            pltpu.VMEM((2, 2 * W, TOK), BF16),
            pltpu.VMEM((512, 2 * H), BF16),
            pltpu.VMEM((512, H), BF16),
            pltpu.VMEM((2, 16, 2, TOK), F32),
            pltpu.VMEM((2, 16, 2, TOK), F32),
            pltpu.VMEM((NCH, 2, CAP, 2 * W), BF16),
            pltpu.VMEM((NCH, 2, CAP, 2 * W), BF16),
            pltpu.VMEM((NCH, 4, 2, RY, BW), BF16),
            pltpu.VMEM((NCH, 2, RY, BW), BF16),
            pltpu.VMEM((NCH, 4, RY, BW), BF16),
            pltpu.VMEM((NCH, RY, BW), BF16),
            pltpu.VMEM((NCH, RY, BW), BF16),
            pltpu.VMEM((NCH, 4, 2, RY, BW), BF16),
            pltpu.VMEM((NCH, 2, 4, RX, BW), BF16),
            pltpu.VMEM((NCH, 4, RX, BW), BF16),
            pltpu.VMEM((NCH, RX, BW), BF16),
            pltpu.VMEM((NCH, 2, RX, BW), BF16),
            pltpu.VMEM((NCH, 2, 4, RX, BW), BF16),
            pltpu.VMEM((NCH, 2, CAP, 2 * W), BF16),
            pltpu.VMEM((NCH, 2, CAP, 2 * W), BF16),
            pltpu.VMEM((2 * W, 2 * BATCH * ROWS), BF16),
            pltpu.VMEM((512, 2 * H), F32),
            pltpu.VMEM((512, H), F32),
            pltpu.VMEM((2, 512, TOK), F32),
            pltpu.VMEM((2, 512, TOK), F32),
            pltpu.VMEM((8, TOK), jnp.int32),
            pltpu.VMEM((8, TOK), F32),
            pltpu.VMEM((2 * W, TOK), BF16),
            pltpu.VMEM((2 * W, TOK), BF16),
            dma((4,)),
            dma((4,)),
            dma((4,)),
            dma((NCH, 24)),
            dma((NCH, 24)),
        ],
        compiler_params=pltpu.CompilerParams(
            collective_id=0, has_side_effects=True, vmem_limit_bytes=57 << 20
        ),
    )(tokens.T, cotangent.T, routing.T, gate_weights.T, w_in[0], w_out[0].T)
    return mixed.T, tgrad.T, wig[None], wog.T[None]


def solution(mesh):
    placed = (
        P("expert", ("pipe", "dp")),
        P("expert", None),
        P("expert", None),
        P("expert", ("pipe", "dp")),
        P("expert", ("pipe", "dp"), None),
        P("expert", None, ("pipe", "dp")),
    )
    return jax.shard_map(
        shards,
        mesh=mesh,
        in_specs=placed,
        out_specs=(
            P("expert", ("pipe", "dp")),
            P("expert", ("pipe", "dp")),
            P("expert", ("pipe", "dp"), None),
            P("expert", None, ("pipe", "dp")),
        ),
        check_vma=False,
    )
```
